256 devices in a mesh: seq: 32 (over z, y), cache: 4 (over x), mp: 2 (over core).
Axes of the slice: x: 4, y: 4, z: 8, core: 2. Of those that a mesh axis runs over, the one named last changes fastest.
Arguments:
- tokens: bfloat16 [12288, 3072], P('seq'), as said below
- query_weight: bfloat16 [3072, 2048], P(None, ('cache', 'mp')), as said below
- key_weight: bfloat16 [3072, 2048], P(None, ('cache', 'mp')), as said below
- value_weight: bfloat16 [3072, 2048], P(None, ('cache', 'mp')), may hold values from -0.109375 to 0.109375
- output_weight: bfloat16 [2048, 3072], P(('cache', 'mp')), may hold values from -1.5 to 1.5
- adapter_down_maps: bfloat16 [8, 3072, 128], P('cache'), may hold values from -0.109375 to 0.109375
- adapter_up_maps: bfloat16 [8, 2, 64, 2048], P('cache'), may hold values from -0.75 to 0.75
- request_lengths: int32 [16], replicated, may hold values from 1 to 6528, 12288 in all
- request_adapter: int32 [16], replicated, may hold values from 0 to 7
- adapter_slot: int32 [8], replicated, may hold values from 0 to 7, each once
Outputs:
- attn_out: bfloat16 [12288, 3072], P('seq', ('cache', 'mp'))
The draws below stay inside these ranges and needn't reach their ends.
Inputs may be any that keep to these rules, and one draw needn't show every extreme that they name: `tokens`: values of order one. `query_weight`: entries of order 1 / sqrt(3072). `key_weight`: entries of order 1 / sqrt(3072). `request_lengths`: the 16 lengths sum to 12288; the longest is exactly 6528. `adapter_slot`: each slot holds exactly one adapter.
All inputs are finite; a program needn't handle non-finite values.
Results may differ from the reference program's by a relative error of at most 0.02.
Values may be sent and summed in bfloat16 or wider, within the bound.
No kernel may reach another device: no remote copies, remote signals or barrier semaphores. Data moves between devices by JAX's collectives and lax.ppermute only.
A program may use at most 128 MiB of HBM per device.

```python
import math
import jax
import jax.numpy as jnp
import numpy as np
from jax import lax

MODEL_WIDTH = 3072
HEAD = 128
HEADS = 16
PROJECTED_WIDTH = 2048
ADAPTER_RANK = 64
ADAPTER_SLOTS = 8
REQS = 16
ROWS = 384
TOKENS = 12288
MOST = 6528
N_SEQ = 32


def draw_tokens(key, part):
    base_rows = jax.random.normal(jax.random.fold_in(key, 3), (TOKENS, MODEL_WIDTH), jnp.float32)
    return jnp.clip(base_rows, -36.0, 36.0).astype(jnp.bfloat16)


def projection_pair(key):
    first_key, second_key = jax.random.split(jax.random.fold_in(key, 11))
    first_draw = jax.random.normal(first_key, (MODEL_WIDTH, PROJECTED_WIDTH), jnp.float32) * MODEL_WIDTH ** (-0.5)
    second_draw = jax.random.normal(second_key, (MODEL_WIDTH, PROJECTED_WIDTH), jnp.float32) * MODEL_WIDTH ** (-0.5)
    return (first_draw, second_draw)


def draw_query_weight(key, part):
    first_draw, second_draw = projection_pair(key)
    return first_draw.astype(jnp.bfloat16)


def draw_key_weight(key, part):
    first_draw, second_draw = projection_pair(key)
    return second_draw.astype(jnp.bfloat16)


def with_ends(result, key, smallest, high):
    spot = [jax.random.randint(jax.random.fold_in(key, axis), (), 0, length) for axis, length in enumerate(result.shape)]
    longest = result.shape.index(max(result.shape))
    beside = spot[:longest] + [(spot[longest] + 1) % result.shape[longest]] + spot[longest + 1:]
    return result.at[tuple(spot)].set(smallest).at[tuple(beside)].set(high)


def level_of(key, extent, shards, smallest, top_value):
    gain = 1.0
    for axis_at, parts in shards:
        draws = jax.random.uniform(jax.random.fold_in(jax.random.fold_in(key, 6), axis_at), (parts,), jnp.float32, smallest / len(shards), top_value / len(shards))
        gain = gain * jnp.repeat(jnp.exp(draws), extent[axis_at] // parts).reshape((-1,) + (1,) * (len(extent) - 1 - axis_at))
    return gain


def profile(number_of, total, most, skew):
    weights = [(1 << 20) // math.isqrt(rank ** skew) + 1 for rank in range(2, number_of + 1)]
    rest, given = total - most - (number_of - 1), [1] * (number_of - 1)
    while rest > 0:
        free = [i for i in range(number_of - 1) if given[i] < most]
        whole, budget = sum([weights[i] for i in free]), rest
        for i in free:
            more = min(most - given[i], max(1, budget * weights[i] // whole), rest)
            given[i] = given[i] + more
            rest = rest - more
    return np.array([most] + given)


def ragged_sizes(own_key, count, total, most, skew):
    if count == 2:
        one = jax.random.randint(own_key, (), max(1, total - most), min(most, total - 1) + 1)
        return jnp.stack([one, total - one])
    lengths = jnp.asarray(profile(count, total, most, skew), jnp.int32)
    twos = (count - 1) // 2
    giver, receiver = lengths[1:1 + 2 * twos:2], lengths[2:2 + 2 * twos:2]
    room = jnp.minimum(giver - 1, most - receiver)
    moved = jax.random.randint(jax.random.fold_in(own_key, 1), (twos,), 0, 1 << 20) % (room + 1)
    lengths = lengths.at[1:1 + 2 * twos:2].set(giver - moved).at[2:2 + 2 * twos:2].set(receiver + moved)
    return lengths[jax.random.permutation(jax.random.fold_in(own_key, 2), count)]


def gaussian(stream_key, shape, scale, bound, pieces=(), kind=jnp.bfloat16):
    result = scale * jax.random.normal(stream_key, shape, jnp.float32)
    if pieces:
        result = result * level_of(stream_key, shape, pieces, -0.22, 0.18)
    return jnp.clip(result, -bound, bound).astype(kind)


def setup_inputs(seed: int = 0) -> dict:
    splits = jax.random.split(jax.random.key(seed), 11)
    return {
        "tokens": draw_tokens(jax.random.fold_in(splits[10], 71), 0),
        "query_weight": draw_query_weight(jax.random.fold_in(splits[10], 71), 0),
        "key_weight": draw_key_weight(jax.random.fold_in(splits[10], 71), 0),
        "value_weight": gaussian(splits[3], (MODEL_WIDTH, PROJECTED_WIDTH), MODEL_WIDTH ** -0.5, 0.109375, ((1, 8),)),
        "output_weight": gaussian(splits[4], (PROJECTED_WIDTH, MODEL_WIDTH), (HEAD // 8) ** -0.5, 1.5, ((0, 8),)),
        "adapter_down_maps": gaussian(splits[5], (ADAPTER_SLOTS, MODEL_WIDTH, 2 * ADAPTER_RANK), MODEL_WIDTH ** -0.5, 0.109375, ((0, 4),)),
        "adapter_up_maps": gaussian(splits[6], (ADAPTER_SLOTS, 2, ADAPTER_RANK, PROJECTED_WIDTH), ADAPTER_RANK ** -0.5, 0.75, ((0, 4),)),
        "request_lengths": ragged_sizes(splits[7], REQS, TOKENS, MOST, 2).astype(jnp.int32),
        "request_adapter": with_ends(jax.random.randint(splits[8], (REQS,), 0, ADAPTER_SLOTS), jax.random.fold_in(splits[8], 1), 0, ADAPTER_SLOTS - 1).astype(jnp.int32),
        "adapter_slot": jax.random.permutation(splits[9], ADAPTER_SLOTS).astype(jnp.int32),
    }


NEG = -1.0e30


def reference(tokens, query_weight, key_weight, value_weight, output_weight, adapter_down_maps, adapter_up_maps, request_lengths, request_adapter, adapter_slot):
    req_ends = jnp.cumsum(request_lengths).astype(jnp.int32)
    token_places = jnp.arange(TOKENS, dtype=jnp.int32)
    segment = jnp.sum((token_places[:, None] >= req_ends[None, :]).astype(jnp.int32), axis=1).astype(jnp.int32)
    cache_slot_row = adapter_slot[request_adapter][segment].astype(jnp.int32)
    query_proj = jnp.dot(tokens, query_weight, preferred_element_type=jnp.float32).astype(jnp.bfloat16)

    def down_for(cache_slot_index):
        return jnp.dot(tokens, adapter_down_maps[cache_slot_index], preferred_element_type=jnp.float32).astype(jnp.bfloat16)

    down_maps_every = lax.map(down_for, jnp.arange(ADAPTER_SLOTS, dtype=jnp.int32))
    adapter_rows = down_maps_every[cache_slot_row, token_places]
    key_adapted_sum = jnp.dot(tokens, key_weight, preferred_element_type=jnp.float32)
    value_adapted_sum = jnp.dot(tokens, value_weight, preferred_element_type=jnp.float32)
    for cache_slot_index in range(ADAPTER_SLOTS):
        selected_maps = (cache_slot_row == cache_slot_index)[:, None]
        key_lowered = jnp.where(selected_maps, adapter_rows[:, :ADAPTER_RANK], jnp.zeros_like(adapter_rows[:, :ADAPTER_RANK]))
        value_lowered = jnp.where(selected_maps, adapter_rows[:, ADAPTER_RANK:], jnp.zeros_like(adapter_rows[:, ADAPTER_RANK:]))
        key_adapted_sum = key_adapted_sum + jnp.dot(key_lowered, adapter_up_maps[cache_slot_index, 0], preferred_element_type=jnp.float32)
        value_adapted_sum = value_adapted_sum + jnp.dot(value_lowered, adapter_up_maps[cache_slot_index, 1], preferred_element_type=jnp.float32)
    key_proj = key_adapted_sum.astype(jnp.bfloat16)
    value_proj = value_adapted_sum.astype(jnp.bfloat16)
    query_heads = query_proj.reshape(TOKENS, HEADS, HEAD).transpose(1, 0, 2)
    key_heads = key_proj.reshape(TOKENS, HEADS, HEAD).transpose(1, 0, 2)
    value_heads = value_proj.reshape(TOKENS, HEADS, HEAD).transpose(1, 0, 2)

    def one_head(operands):
        head_query, head_key, head_value = operands

        def one_block(block_start):
            block_query = lax.dynamic_slice_in_dim(head_query, block_start, ROWS, 0)
            block_segment = lax.dynamic_slice_in_dim(segment, block_start, ROWS, 0)
            scores = jnp.dot(block_query, head_key.T, preferred_element_type=jnp.float32) * (HEAD ** -0.5)
            allowed = block_segment[:, None] == segment[None, :]
            scores = jnp.where(allowed, scores, NEG)
            row_top = jnp.max(scores, axis=1, keepdims=True)
            weights = jnp.where(allowed, jnp.exp(scores - row_top), 0.0)
            weight_low = weights.astype(jnp.bfloat16)
            numer = jnp.dot(weight_low, head_value, preferred_element_type=jnp.float32)
            return numer / jnp.sum(weights, axis=1, keepdims=True)

        block_starts = jnp.arange(N_SEQ, dtype=jnp.int32) * ROWS
        return lax.map(one_block, block_starts).reshape(TOKENS, HEAD)

    heads_out = lax.map(one_head, (query_heads, key_heads, value_heads))
    attended = heads_out.transpose(1, 0, 2).reshape(TOKENS, PROJECTED_WIDTH).astype(jnp.bfloat16)
    return jnp.dot(attended, output_weight, preferred_element_type=jnp.float32).astype(jnp.bfloat16)
```

```python
import jax
import jax.numpy as jnp
from jax import lax
from jax.sharding import PartitionSpec as P

HEAD = 128


NEG = -1e30


def segment_of(token_places, req_ends):
    return jnp.sum((token_places[:, None] >= req_ends[None, :]).astype(jnp.int32), axis=1)


def per_device(
    tokens,
    query_weight,
    key_weight,
    value_weight,
    output_weight,
    adapter_down_maps,
    adapter_up_maps,
    request_lengths,
    request_adapter,
    adapter_slot,
):
    row_count = tokens.shape[0]
    col_count = query_weight.shape[1]
    heads_here = col_count // HEAD
    seq_count = lax.axis_size("seq")
    all_tokens = row_count * seq_count
    cache_slot_count = adapter_down_maps.shape[0] * lax.axis_size("cache")
    adapter_rank_size = adapter_down_maps.shape[2] // 2
    request_count = request_lengths.shape[0]
    at_most = jnp.arange(request_count)[:, None] >= jnp.arange(request_count)[None, :]
    req_ends = jnp.sum(jnp.where(at_most, request_lengths[None, :], 0), axis=1)
    seq_first = lax.axis_index("seq") * row_count
    token_places = seq_first + jnp.arange(row_count, dtype=jnp.int32)
    segment = segment_of(token_places, req_ends)
    slot_ids = jnp.arange(cache_slot_count, dtype=jnp.int32)
    adapter_hit = request_adapter[:, None] == slot_ids[None, :]
    slot_req = jnp.sum(jnp.where(adapter_hit, adapter_slot[None, :], 0), axis=1)
    request_hit = segment[:, None] == jnp.arange(request_count, dtype=jnp.int32)[None, :]
    cache_slot_row = jnp.sum(jnp.where(request_hit, slot_req[None, :], 0), axis=1)
    up_maps_block = lax.all_to_all(
        adapter_up_maps, "cache", split_axis=3, concat_axis=0, tiled=True
    )
    up_mine = lax.dynamic_slice_in_dim(
        up_maps_block, lax.axis_index("mp") * col_count, col_count, 3
    )
    down_maps_every = jnp.einsum(
        "td,sdr->str",
        tokens,
        lax.all_gather(adapter_down_maps, "cache", axis=0, tiled=True),
        preferred_element_type=jnp.float32,
    ).astype(jnp.bfloat16)
    chosen = (cache_slot_row[:, None] == slot_ids[None, :]).astype(jnp.bfloat16)
    masked = jnp.transpose(down_maps_every, (1, 0, 2)) * chosen[:, :, None]
    down_key = masked[:, :, :adapter_rank_size].reshape(
        row_count, cache_slot_count * adapter_rank_size
    )
    down_value = masked[:, :, adapter_rank_size:].reshape(
        row_count, cache_slot_count * adapter_rank_size
    )
    up_key = up_mine[:, 0].reshape(cache_slot_count * adapter_rank_size, col_count)
    up_value = up_mine[:, 1].reshape(cache_slot_count * adapter_rank_size, col_count)
    query_proj = jnp.dot(tokens, query_weight, preferred_element_type=jnp.float32).astype(
        jnp.bfloat16
    )
    key_proj = (
        jnp.dot(tokens, key_weight, preferred_element_type=jnp.float32)
        + jnp.dot(down_key, up_key, preferred_element_type=jnp.float32)
    ).astype(jnp.bfloat16)
    value_proj = (
        jnp.dot(tokens, value_weight, preferred_element_type=jnp.float32)
        + jnp.dot(down_value, up_value, preferred_element_type=jnp.float32)
    ).astype(jnp.bfloat16)
    query_heads = query_proj.reshape(row_count, heads_here, HEAD)
    score_scale = HEAD ** (-0.5)

    def absorb(state, key_rows, value_rows, key_segment):
        row_top, row_mass, weighted = state
        key_total = key_rows.shape[0]
        key_heads = key_rows.reshape(key_total, heads_here, HEAD)
        value_heads = value_rows.reshape(key_total, heads_here, HEAD)
        scores = (
            jnp.einsum("qhe,khe->hqk", query_heads, key_heads, preferred_element_type=jnp.float32)
            * score_scale
        )
        allowed = (segment[:, None] == key_segment[None, :])[None]
        scores = jnp.where(allowed, scores, NEG)
        new_top = jnp.maximum(row_top, jnp.max(scores, axis=2))
        weights = jnp.where(allowed, jnp.exp(scores - new_top[:, :, None]), 0.0)
        factor = jnp.exp(row_top - new_top)
        row_mass = row_mass * factor + jnp.sum(weights, axis=2)
        weight_low = weights.astype(jnp.bfloat16)
        weighted = weighted * factor[:, :, None] + jnp.einsum(
            "hqk,khe->hqe", weight_low, value_heads, preferred_element_type=jnp.float32
        )
        return (new_top, row_mass, weighted)

    def visit_keys(state, key_rows, value_rows, key_first):
        key_total = key_rows.shape[0]
        key_positions = key_first + jnp.arange(key_total, dtype=jnp.int32)
        inside = (key_positions >= 0) & (key_positions < all_tokens)
        key_segment = jnp.where(inside, segment_of(key_positions, req_ends), -1)
        return absorb(state, key_rows, value_rows, key_segment)

    initial = (
        jnp.full((heads_here, row_count), NEG, jnp.float32),
        jnp.zeros((heads_here, row_count), jnp.float32),
        jnp.zeros((heads_here, row_count, HEAD), jnp.float32),
    )
    state = initial
    key_part = lax.all_gather(key_proj, "seq", axis=0, tiled=True)
    value_part = lax.all_gather(value_proj, "seq", axis=0, tiled=True)
    key_total = key_part.shape[0]
    block_count = key_total // row_count

    def scan_step(current, block_item):
        key_block, value_block, block_index = block_item
        return (visit_keys(current, key_block, value_block, block_index * row_count), None)

    state, unused = lax.scan(
        scan_step,
        state,
        (
            key_part.reshape(block_count, row_count, col_count),
            value_part.reshape(block_count, row_count, col_count),
            jnp.arange(block_count, dtype=jnp.int32),
        ),
    )
    final_top, final_mass, weighted = state
    attended = (
        (weighted / final_mass[:, :, None])
        .transpose(1, 0, 2)
        .reshape(row_count, col_count)
        .astype(jnp.bfloat16)
    )
    partial_out = jnp.dot(attended, output_weight, preferred_element_type=jnp.float32)
    return lax.psum_scatter(
        partial_out.astype(jnp.bfloat16), ("cache", "mp"), scatter_dimension=1, tiled=True
    )


def solution(mesh):
    placed = (
        P("seq", None),
        P(None, ("cache", "mp")),
        P(None, ("cache", "mp")),
        P(None, ("cache", "mp")),
        P(("cache", "mp"), None),
        P("cache", None, None),
        P("cache", None, None, None),
        P(),
        P(),
        P(),
    )
    return jax.shard_map(
        per_device, mesh=mesh, in_specs=placed, out_specs=P("seq", ("cache", "mp")), check_vma=False
    )
```

```python
import functools
import math

import jax
import jax.numpy as jnp
from jax import lax
from jax.experimental import pallas as pl
from jax.experimental.pallas import tpu as pltpu
from jax.sharding import PartitionSpec as P

HEAD = 128
SEQ_Z = 8
SEQ_Y = 4
CACHE = 4
START = -1e30
NEG = -3e30
TAIL = 16
QUERY_SCALE = HEAD ** (-0.5) * math.log2(math.e)


def around_z(step):
    return [
        (z * SEQ_Y + y, (z + step) % SEQ_Z * SEQ_Y + y) for z in range(SEQ_Z) for y in range(SEQ_Y)
    ]


def around_y(step):
    return [
        (z * SEQ_Y + y, z * SEQ_Y + (y + step) % SEQ_Y) for z in range(SEQ_Z) for y in range(SEQ_Y)
    ]


def around_x(step):
    return [(x, (x + step) % CACHE) for x in range(CACHE)]


def other_core(array):
    return lax.ppermute(array, "mp", [(0, 1), (1, 0)])


def matmul(a, b):
    return lax.dot_general(a, b, (((1,), (0,)), ((), ())), preferred_element_type=jnp.float32)


def attend_kernel(first, last, by_head, block_total, *refs):
    info, queries, span = refs[0], refs[1], refs[2]
    at = 3
    blocks = []
    for _ in range(block_total):
        width = 4 if by_head else 2
        blocks.append(refs[at : at + width])
        at += width
    if not first:
        state_in, sums_in = refs[at : at + 2]
        at += 2
    outs = refs[at:]
    group, head = pl.program_id(0), pl.program_id(1)
    if last:
        state, sums = outs[-2:]
        outs = outs[:-2]
    else:
        state, sums = outs
    if first:
        state[...] = jnp.zeros(state.shape, jnp.float32)
        sums[0:1, :] = jnp.full((1, sums.shape[1]), START, jnp.float32)
        sums[1:2, :] = jnp.zeros((1, sums.shape[1]), jnp.float32)
    else:
        state[...] = state_in[...]
        sums[...] = sums_in[...]
    query_first, query_last = info[2 * group], info[2 * group + 1]
    row_total = queries.shape[1]
    for which, block in enumerate(blocks):
        base = 8 + 3 * which
        key_first, key_last, key_row = info[base], info[base + 1], info[base + 2]

        def visit(masked):
            if by_head:
                keys = jnp.where(head == 0, block[0][...], block[1][...])
                values = jnp.where(head == 0, block[2][...], block[3][...])
            else:
                keys, values = block[0][head], block[1][head]
            for part in range(row_total // 128):
                cols = slice(part * 128, part * 128 + 128)
                scores = matmul(keys, queries[:, cols])
                if masked:
                    places = key_row + lax.broadcasted_iota(jnp.int32, scores.shape, 0)
                    inside = (places >= span[0:1, cols]) & (places < span[1:2, cols])
                    scores = jnp.where(inside, scores, NEG)
                old = sums[0:1, cols]
                top = jnp.maximum(old, jnp.max(scores, axis=0, keepdims=True))
                weights = jnp.exp2(scores - top)
                factor = jnp.exp2(old - top)
                sums[0:1, cols] = top
                sums[1:2, cols] = sums[1:2, cols] * factor + jnp.sum(weights, axis=0, keepdims=True)
                state[:, cols] = state[:, cols] * factor + matmul(values, weights.astype(jnp.bfloat16))

        meets = (key_first <= query_last) & (key_last >= query_first)
        whole = (key_first == key_last) & (query_first == query_last) & (key_first == query_first)

        @pl.when(meets & whole)
        def _():
            visit(False)

        @pl.when(meets & jnp.logical_not(whole))
        def _():
            visit(True)

    if last:
        mass = sums[1:2, :]
        some = mass > 0.0
        result = (state[...] / jnp.where(some, mass, 1.0)).astype(jnp.bfloat16)
        logs = jnp.where(some, sums[0:1, :] + jnp.log2(jnp.where(some, mass, 1.0)), START)
        high = logs.astype(jnp.bfloat16)
        low = (logs - high.astype(jnp.float32)).astype(jnp.bfloat16)
        rows = lax.broadcasted_iota(jnp.int32, (TAIL, row_total), 0)
        tail = jnp.where(rows == 0, high.astype(jnp.float32), low.astype(jnp.float32)).astype(jnp.bfloat16)
        for place, out in enumerate(outs):

            @pl.when(group == place)
            def _(out=out):
                out[0:HEAD, :] = result
                out[HEAD : HEAD + TAIL, :] = tail


def attend(info, queries, spans, blocks, state, last=False):
    first = state is None
    by_head = len(blocks[0]) == 4
    groups, heads, _, row_total = queries.shape
    per_query = lambda rows: pl.BlockSpec((None, None, rows, row_total), lambda g, h, s: (g, h, 0, 0))
    in_specs = [per_query(HEAD), pl.BlockSpec((None, 8, row_total), lambda g, h, s: (g, 0, 0))]
    operands = [queries, spans]
    for block in blocks:
        for array in block:
            in_specs.append(pl.BlockSpec(array.shape, lambda g, h, s, rank=array.ndim: (0,) * rank))
            operands.append(array)
    if not first:
        in_specs += [per_query(HEAD), per_query(8)]
        operands += list(state)
    state_shapes = [
        jax.ShapeDtypeStruct((groups, heads, HEAD, row_total), jnp.float32),
        jax.ShapeDtypeStruct((groups, heads, 8, row_total), jnp.float32),
    ]
    scratch = []
    if last:
        def place(group):
            def index(g, h, s):
                return (jnp.where(g == group, h, jnp.where(g < group, 0, heads - 1)), 0, 0)

            return index

        out_shape = [jax.ShapeDtypeStruct((heads, HEAD + TAIL, row_total), jnp.bfloat16)] * groups
        out_specs = [
            pl.BlockSpec((None, HEAD + TAIL, row_total), place(group)) for group in range(groups)
        ]
        scratch = [pltpu.VMEM((HEAD, row_total), jnp.float32), pltpu.VMEM((8, row_total), jnp.float32)]
    else:
        out_shape, out_specs = state_shapes, [per_query(HEAD), per_query(8)]
    madds = groups * heads * row_total * row_total * HEAD * 2 * len(blocks)
    return pl.pallas_call(
        functools.partial(attend_kernel, first, last, by_head, len(blocks)),
        grid_spec=pltpu.PrefetchScalarGridSpec(
            num_scalar_prefetch=1,
            grid=(groups, heads),
            in_specs=in_specs,
            out_specs=out_specs,
            scratch_shapes=scratch,
        ),
        out_shape=out_shape,
        compiler_params=pltpu.CompilerParams(vmem_limit_bytes=40 * 2**20),
        cost_estimate=pl.CostEstimate(
            flops=2 * madds, bytes_accessed=4 * 2**20, transcendentals=madds // HEAD // 2
        ),
    )(info, *operands)


def merge_kernel(*refs):
    out, parts = refs[-1], refs[:-1]
    logs = [
        part[HEAD : HEAD + 1, :].astype(jnp.float32) + part[HEAD + 1 : HEAD + 2, :].astype(jnp.float32)
        for part in parts
    ]
    top = functools.reduce(jnp.maximum, logs)
    shares = [jnp.exp2(log - top) for log in logs]
    mass = functools.reduce(jnp.add, shares)
    total = functools.reduce(
        jnp.add, [part[0:HEAD, :].astype(jnp.float32) * share for part, share in zip(parts, shares)]
    )
    out[...] = (total / mass).astype(jnp.bfloat16)


def merge(parts):
    heads, rows, row_total = parts[0].shape
    return pl.pallas_call(
        merge_kernel,
        grid=(heads,),
        in_specs=[pl.BlockSpec((None, rows, row_total), lambda h: (h, 0, 0))] * len(parts),
        out_specs=pl.BlockSpec((None, HEAD, row_total), lambda h: (h, 0, 0)),
        out_shape=jax.ShapeDtypeStruct((heads, HEAD, row_total), jnp.bfloat16),
        cost_estimate=pl.CostEstimate(flops=10**6, bytes_accessed=2**20, transcendentals=0),
    )(*parts)


def per_device(
    tokens,
    query_weight,
    key_weight,
    value_weight,
    output_weight,
    adapter_down_maps,
    adapter_up_maps,
    request_lengths,
    request_adapter,
    adapter_slot,
):
    row_count, width = tokens.shape
    col_count = query_weight.shape[1]
    heads_here = col_count // HEAD
    slots_here = adapter_down_maps.shape[0]
    rank = adapter_down_maps.shape[2] // 2
    request_count = request_lengths.shape[0]
    out_cols = output_weight.shape[1] // (2 * CACHE)
    seq, cache, core = lax.axis_index("seq"), lax.axis_index("cache"), lax.axis_index("mp")
    seq_z, seq_y = seq // SEQ_Y, seq % SEQ_Y
    requests = jnp.arange(request_count, dtype=jnp.int32)
    before = requests[:, None] > requests[None, :]
    starts = jnp.sum(jnp.where(before, request_lengths[None, :], 0), axis=1)
    ends = starts + request_lengths
    slot_ids = jnp.arange(adapter_slot.shape[0], dtype=jnp.int32)
    slot_of_request = jnp.sum(
        jnp.where(request_adapter[:, None] == slot_ids[None, :], adapter_slot[None, :], 0), axis=1
    )

    def request_at(places):
        return jnp.sum((places[..., None] >= ends).astype(jnp.int32), axis=-1)

    def of_request(values, places):
        inside = (places[..., None] >= starts) & (places[..., None] < ends)
        return jnp.sum(jnp.where(inside, values, 0), axis=-1)

    my_places = seq * row_count + jnp.arange(row_count, dtype=jnp.int32)
    my_slots = of_request(slot_of_request, my_places)

    def up_columns(cache_to):
        return lax.dynamic_slice_in_dim(adapter_up_maps, (cache_to * 2 + core) * col_count, col_count, 3)

    ups = [up_columns(cache)] + [
        lax.ppermute(up_columns((cache + step) % CACHE), "cache", around_x(step)) for step in (1, 2, 3)
    ]
    lowered = jnp.einsum(
        "td,sdr->str", tokens, adapter_down_maps, preferred_element_type=jnp.float32
    ).astype(jnp.bfloat16)
    own_lowered = jnp.zeros_like(lowered[0])
    for slot in range(slots_here):
        mine = my_slots == cache * slots_here + slot
        own_lowered = jnp.where(mine[:, None], lowered[slot], own_lowered)
    low_rows = own_lowered
    for step in (2, 1, 3):
        low_rows = low_rows + lax.ppermute(own_lowered, "cache", around_x(step))
    masks = [
        my_slots == (cache + CACHE - step) % CACHE * slots_here + slot
        for step in range(CACHE)
        for slot in range(slots_here)
    ]
    key_low = jnp.concatenate([jnp.where(m[:, None], low_rows[:, :rank], 0) for m in masks], axis=1)
    value_low = jnp.concatenate([jnp.where(m[:, None], low_rows[:, rank:], 0) for m in masks], axis=1)
    up_key = jnp.concatenate([up[:, 0].reshape(-1, col_count) for up in ups], axis=0)
    up_value = jnp.concatenate([up[:, 1].reshape(-1, col_count) for up in ups], axis=0)

    query = jnp.dot(tokens, query_weight, preferred_element_type=jnp.float32)
    query = (query * QUERY_SCALE).astype(jnp.bfloat16).T.reshape(heads_here, HEAD, row_count)
    key = (
        jnp.dot(tokens, key_weight, preferred_element_type=jnp.float32)
        + jnp.dot(key_low, up_key, preferred_element_type=jnp.float32)
    ).astype(jnp.bfloat16)
    key = key.reshape(row_count, heads_here, HEAD).transpose(1, 0, 2)
    value = (
        jnp.dot(tokens, value_weight, preferred_element_type=jnp.float32)
        + jnp.dot(value_low, up_value, preferred_element_type=jnp.float32)
    ).astype(jnp.bfloat16)
    value = value.T.reshape(heads_here, HEAD, row_count)

    queries = [query] + [lax.ppermute(query, "seq", around_y(step)) for step in (1, 2, 3)]
    queries = jnp.stack(queries)
    group_ids = jnp.arange(SEQ_Y, dtype=jnp.int32)
    group_rows = (seq_z * SEQ_Y + (seq_y + SEQ_Y - group_ids) % SEQ_Y) * row_count
    query_places = group_rows[:, None] + jnp.arange(row_count, dtype=jnp.int32)[None, :]
    spans = jnp.stack([of_request(starts, query_places), of_request(ends, query_places)], axis=1)
    spans = jnp.pad(spans, ((0, 0), (0, 6), (0, 0)))
    query_info = jnp.stack(
        [request_at(group_rows), request_at(group_rows + row_count - 1)], axis=1
    ).reshape(-1)

    def info_of(steps):
        rows = jnp.stack([((seq_z + SEQ_Z - s) % SEQ_Z * SEQ_Y + seq_y) * row_count for s in steps])
        keys = jnp.stack([request_at(rows), request_at(rows + row_count - 1), rows], axis=1)
        return jnp.concatenate([query_info, keys.reshape(-1)])

    key_right = key_left = key
    value_right = value_left = value
    state = attend(info_of([0]), queries, spans, [(key, value)], None)
    for step in range(1, SEQ_Z // 2):
        key_right = lax.ppermute(key_right, "seq", around_z(1))
        key_left = lax.ppermute(key_left, "seq", around_z(-1))
        value_right = lax.ppermute(value_right, "seq", around_z(1))
        value_left = lax.ppermute(value_left, "seq", around_z(-1))
        state = attend(
            info_of([step, -step]),
            queries,
            spans,
            [(key_right, value_right), (key_left, value_left)],
            state,
        )
    far = (
        lax.ppermute(key_right[0], "seq", around_z(1)),
        lax.ppermute(key_left[1], "seq", around_z(-1)),
        lax.ppermute(value_right[0], "seq", around_z(1)),
        lax.ppermute(value_left[1], "seq", around_z(-1)),
    )
    parts = attend(info_of([SEQ_Z // 2]), queries, spans, [far], state, last=True)

    output_weight, _ = lax.optimization_barrier((output_weight, key))

    def out_columns(cache_to, core_to):
        return lax.dynamic_slice_in_dim(output_weight, (cache_to * 2 + core_to) * out_cols, out_cols, 1)

    weight_rows = []
    for step in range(CACHE):
        pair = jnp.stack(
            [out_columns((cache + step) % CACHE, core), out_columns((cache + step) % CACHE, 1 - core)]
        )
        weight_rows.append(lax.ppermute(pair, "cache", around_x(step)) if step else pair)
    weight_same = jnp.concatenate([pair[0] for pair in weight_rows])
    weight_other = other_core(jnp.concatenate([pair[1] for pair in weight_rows]))

    parts = [parts[0]] + [lax.ppermute(parts[g], "seq", around_y(-g)) for g in (2, 1, 3)]
    attended = merge(parts).reshape(col_count, row_count)
    heads_same = [attended] + [lax.ppermute(attended, "cache", around_x(step)) for step in (1, 2, 3)]
    heads_same = jnp.concatenate(heads_same)
    heads_other = other_core(heads_same)
    contract = (((0,), (0,)), ((), ()))
    return (
        lax.dot_general(heads_same, weight_same, contract, preferred_element_type=jnp.float32)
        + lax.dot_general(heads_other, weight_other, contract, preferred_element_type=jnp.float32)
    ).astype(jnp.bfloat16)


def solution(mesh):
    placed = (
        P("seq", None),
        P(None, ("cache", "mp")),
        P(None, ("cache", "mp")),
        P(None, ("cache", "mp")),
        P(("cache", "mp"), None),
        P("cache", None, None),
        P("cache", None, None, None),
        P(),
        P(),
        P(),
    )
    return jax.shard_map(
        per_device, mesh=mesh, in_specs=placed, out_specs=P("seq", ("cache", "mp")), check_vma=False
    )
```

```python
import functools
import math

import jax
import jax.numpy as jnp
from jax import lax
from jax.experimental import pallas as pl
from jax.experimental.pallas import tpu as pltpu
from jax.sharding import PartitionSpec as P

HEAD = 128
SEQ_Z = 8
SEQ_Y = 4
CACHE = 4
START = -1e30
NEG = -3e30
TAIL = 16
QUERY_SCALE = HEAD ** (-0.5) * math.log2(math.e)


ATTEND_FLOPS = 10**9


def around_z(step):
    return [
        (z * SEQ_Y + y, (z + step) % SEQ_Z * SEQ_Y + y) for z in range(SEQ_Z) for y in range(SEQ_Y)
    ]


def around_y(step):
    return [
        (z * SEQ_Y + y, z * SEQ_Y + (y + step) % SEQ_Y) for z in range(SEQ_Z) for y in range(SEQ_Y)
    ]


def around_x(step):
    return [(x, (x + step) % CACHE) for x in range(CACHE)]


def matmul(a, b, dims=((1,), (0,))):
    return lax.dot_general(a, b, (dims, ((), ())), preferred_element_type=jnp.float32)


def whole(shape):
    return pl.BlockSpec(shape, lambda *at: (0,) * len(shape))


def request_ends(lengths):
    bounds, at = [], jnp.int32(0)
    for r in range(lengths.shape[0]):
        bounds.append((at, at + lengths[r]))
        at = at + lengths[r]
    return bounds


def slots_of_rows(places, lengths, adapters, slots):
    found = jnp.zeros(places.shape, jnp.int32)
    for r, (start, _) in enumerate(request_ends(lengths)):
        found = jnp.where(places >= start, slots[adapters[r]], found)
    return found


def lower_kernel(steps, where, lengths, adapters, slots, tokens, down, *refs):
    ups, outs, total = refs[:CACHE], refs[CACHE:-1], refs[-1]
    step = pl.program_id(0)
    row_total, low = tokens.shape[0], down.shape[2]

    @pl.when(step == 0)
    def _():
        total[...] = jnp.zeros(total.shape, jnp.float32)

    for slot in range(down.shape[0]):
        total[:, slot * low : (slot + 1) * low] += matmul(tokens[...], down[slot])

    @pl.when(step == steps - 1)
    def _():
        places = where[0] * row_total + lax.broadcasted_iota(jnp.int32, (row_total, low), 0)
        mine = slots_of_rows(places, lengths, adapters, slots)
        rows = jnp.zeros((row_total, low), jnp.float32)
        for slot in range(down.shape[0]):
            held = total[:, slot * low : (slot + 1) * low]
            rows = jnp.where(mine == where[1] * down.shape[0] + slot, held, rows)
        rows = rows.astype(jnp.bfloat16)
        for up, out in zip(ups, outs):
            out[0:row_total, :] = rows
            up_rows = up.shape[0]
            for half in range(up.shape[1] // HEAD):
                at = row_total + half * up_rows
                out[at : at + up_rows, :] = up[:, half * HEAD : (half + 1) * HEAD]


def lower(where, lengths, adapters, slots, tokens, down, ups, col_count):
    steps = 3
    row_total, width = tokens.shape
    slot_total, _, low = down.shape
    up_rows = ups.shape[0]
    deep = width // steps
    out_rows = row_total + up_rows * col_count // HEAD

    def columns(step):
        return lambda i, where, *rest: (0, lax.rem(where[1] + step, CACHE) * 2 + where[2])

    return pl.pallas_call(
        functools.partial(lower_kernel, steps),
        grid_spec=pltpu.PrefetchScalarGridSpec(
            num_scalar_prefetch=4,
            grid=(steps,),
            in_specs=[
                pl.BlockSpec((row_total, deep), lambda i, *rest: (0, i)),
                pl.BlockSpec((slot_total, deep, low), lambda i, *rest: (0, i, 0)),
            ]
            + [pl.BlockSpec((up_rows, col_count), columns(step)) for step in range(CACHE)],
            out_specs=[whole((out_rows, HEAD))] * CACHE,
            scratch_shapes=[pltpu.VMEM((row_total, slot_total * low), jnp.float32)],
        ),
        out_shape=[jax.ShapeDtypeStruct((out_rows, HEAD), jnp.bfloat16)] * CACHE,
        compiler_params=pltpu.CompilerParams(vmem_limit_bytes=62 * 2**20),
        cost_estimate=pl.CostEstimate(flops=6 * 10**8, bytes_accessed=6 * 2**20, transcendentals=0),
    )(where, lengths, adapters, slots, tokens, down, *[ups] * CACHE)


def project_kernel(steps, where, lengths, tokens, wq, wk, wv, query, key, value, spans, info, total):
    step = pl.program_id(0)
    row_total = tokens.shape[0]
    held = tokens[...]

    @pl.when(step == 0)
    def _():
        total[...] = matmul(held, wq[...])
        key[...] = matmul(held, wk[...])
        value[...] = matmul(held, wv[...])
        bounds = request_ends(lengths)
        seq = where[0]
        seq_z, seq_y = lax.div(seq, SEQ_Y), lax.rem(seq, SEQ_Y)

        def request_at(row):
            found = jnp.int32(0)
            for _, end in bounds:
                found = found + (row >= end).astype(jnp.int32)
            return found

        def groups_row(group):
            return (seq_z * SEQ_Y + lax.rem(seq_y + SEQ_Y - group, SEQ_Y)) * row_total

        for group in range(SEQ_Y):
            row = groups_row(group)
            info[2 * group] = request_at(row)
            info[2 * group + 1] = request_at(row + row_total - 1)
            places = row + lax.broadcasted_iota(jnp.int32, (8, row_total), 1)
            starts = jnp.zeros(places.shape, jnp.int32)
            ends = jnp.zeros(places.shape, jnp.int32)
            for start, end in bounds:
                starts = jnp.where(places >= start, start, starts)
                ends = jnp.where(places >= start, end, ends)
            index = lax.broadcasted_iota(jnp.int32, (8, row_total), 0)
            cols = slice(group % 2 * row_total, group % 2 * row_total + row_total)
            spans[group // 2, :, cols] = jnp.where(index == 0, starts, ends)
        for back in range(SEQ_Z):
            row = (lax.rem(seq_z + SEQ_Z - back, SEQ_Z) * SEQ_Y + seq_y) * row_total
            info[8 + 3 * back] = request_at(row)
            info[8 + 3 * back + 1] = request_at(row + row_total - 1)
            info[8 + 3 * back + 2] = row

    @pl.when(step > 0)
    def _():
        total[...] += matmul(held, wq[...])
        key[...] += matmul(held, wk[...])
        value[...] += matmul(held, wv[...])

    @pl.when(step == steps - 1)
    def _():
        scaled = total[...] * QUERY_SCALE
        for head in range(query.shape[0]):
            query[head] = scaled[:, head * HEAD : (head + 1) * HEAD].T.astype(jnp.bfloat16)


def project(where, lengths, tokens, wq, wk, wv):
    steps = 3
    row_total, width = tokens.shape
    col_count = wq.shape[1]
    heads = col_count // HEAD
    deep = width // steps
    weight = pl.BlockSpec((deep, col_count), lambda i, *rest: (i, 0))
    summed = jax.ShapeDtypeStruct((row_total, col_count), jnp.float32)
    return pl.pallas_call(
        functools.partial(project_kernel, steps),
        grid_spec=pltpu.PrefetchScalarGridSpec(
            num_scalar_prefetch=2,
            grid=(steps,),
            in_specs=[pl.BlockSpec((row_total, deep), lambda i, *rest: (0, i)), weight, weight, weight],
            out_specs=[
                whole((heads, HEAD, row_total)),
                whole((row_total, col_count)),
                whole((row_total, col_count)),
                whole((SEQ_Y // 2, 8, 2 * row_total)),
                pl.BlockSpec(memory_space=pltpu.SMEM),
            ],
            scratch_shapes=[pltpu.VMEM((row_total, col_count), jnp.float32)],
        ),
        out_shape=[
            jax.ShapeDtypeStruct((heads, HEAD, row_total), jnp.bfloat16),
            summed,
            summed,
            jax.ShapeDtypeStruct((SEQ_Y // 2, 8, 2 * row_total), jnp.int32),
            jax.ShapeDtypeStruct((8 + 3 * SEQ_Z,), jnp.int32),
        ],
        compiler_params=pltpu.CompilerParams(vmem_limit_bytes=62 * 2**20),
        cost_estimate=pl.CostEstimate(flops=18 * 10**8, bytes_accessed=8 * 2**20, transcendentals=0),
    )(where, lengths, tokens, wq, wk, wv)


def adapt_kernel(slot_total, where, lengths, adapters, slots, key, value, *refs):
    messages, out = refs[:-1], refs[-1]
    row_total = key.shape[0]
    low = functools.reduce(jnp.add, [m[0:row_total, :].astype(jnp.float32) for m in messages])
    places = where[0] * row_total + lax.broadcasted_iota(jnp.int32, low.shape, 0)
    mine = slots_of_rows(places, lengths, adapters, slots)
    for_key = lax.broadcasted_iota(jnp.int32, low.shape, 1) < low.shape[1] // 2
    key_low, value_low = [], []
    for step in range(len(messages)):
        for slot in range(slot_total):
            holder = lax.rem(where[1] + CACHE - step, CACHE) * slot_total + slot
            rows = jnp.where(mine == holder, low, 0.0)
            key_low.append(jnp.where(for_key, rows, 0.0).astype(jnp.bfloat16))
            value_low.append(jnp.where(for_key, 0.0, rows).astype(jnp.bfloat16))
    key_low, value_low = jnp.concatenate(key_low, axis=1), jnp.concatenate(value_low, axis=1)
    up_rows = slot_total * low.shape[1]
    for head in range(out.shape[0]):
        cols = slice(head * HEAD, (head + 1) * HEAD)
        at = row_total + head * up_rows
        up = jnp.concatenate([m[at : at + up_rows, :] for m in messages], axis=0)
        out[head, 0:row_total, :] = (key[:, cols] + matmul(key_low, up)).astype(jnp.bfloat16)
        summed = value[:, cols] + matmul(value_low, up)
        for part in range(row_total // HEAD):
            rows = slice(part * HEAD, (part + 1) * HEAD)
            out[head, row_total + part * HEAD : row_total + (part + 1) * HEAD, :] = summed[
                rows, :
            ].T.astype(jnp.bfloat16)


def adapt(where, lengths, adapters, slots, key, value, messages, slot_total):
    row_total, col_count = key.shape
    heads = col_count // HEAD
    return pl.pallas_call(
        functools.partial(adapt_kernel, slot_total),
        grid_spec=pltpu.PrefetchScalarGridSpec(
            num_scalar_prefetch=4,
            grid=(1,),
            in_specs=[whole(a.shape) for a in (key, value, *messages)],
            out_specs=whole((heads, 2 * row_total, HEAD)),
        ),
        out_shape=jax.ShapeDtypeStruct((heads, 2 * row_total, HEAD), jnp.bfloat16),
        compiler_params=pltpu.CompilerParams(vmem_limit_bytes=40 * 2**20),
        cost_estimate=pl.CostEstimate(flops=4 * 10**8, bytes_accessed=2 * 2**20, transcendentals=0),
    )(where, lengths, adapters, slots, key, value, *messages)


def attend_kernel(first, last, backs, info, queries, span, *refs):
    at = 0
    blocks = []
    for back in backs:
        width = 2 if back == SEQ_Z // 2 else 1
        blocks.append(refs[at : at + width])
        at += width
    if not first:
        state_in, sums_in = refs[at : at + 2]
        at += 2
    outs = refs[at:]
    state, sums = outs[-2:]
    outs = outs[:-2]
    pair, head = pl.program_id(0), pl.program_id(1)
    columns = queries.shape[1]
    row_total = columns // 2
    if first:
        state[...] = jnp.zeros(state.shape, jnp.float32)
        sums[0:1, :] = jnp.full((1, columns), START, jnp.float32)
        sums[1:2, :] = jnp.zeros((1, columns), jnp.float32)
    else:
        state[...] = state_in[...]
        sums[...] = sums_in[...]
    a_first, a_last = info[4 * pair], info[4 * pair + 1]
    b_first, b_last = info[4 * pair + 2], info[4 * pair + 3]
    for back, block in zip(backs, blocks):
        base = 8 + 3 * back
        key_first, key_last, key_row = info[base], info[base + 1], info[base + 2]

        def visit(masked, block=block, key_row=key_row):
            if len(block) == 2:
                packed = jnp.where(head == 0, block[0][...], block[1][...])
            else:
                packed = block[0][head]
            keys = packed[0:row_total]
            values = jnp.concatenate(
                [packed[row_total + p * HEAD : row_total + (p + 1) * HEAD] for p in range(row_total // HEAD)],
                axis=1,
            )
            index = lax.broadcasted_iota(jnp.int32, (TAIL, row_total), 0)
            ones = jnp.where(index == 0, 1.0, 0.0).astype(jnp.bfloat16)
            values = jnp.concatenate([values, ones], axis=0)
            chains = [slice(at, at + 256) for at in range(0, columns, 256)]
            scores = [matmul(keys, queries[:, cols]) for cols in chains]
            weights = []
            for score, cols in zip(scores, chains):
                if masked:
                    places = key_row + lax.broadcasted_iota(jnp.int32, score.shape, 0)
                    inside = (places >= span[0:1, cols]) & (places < span[1:2, cols])
                    score = jnp.where(inside, score, NEG)
                old = sums[0:1, cols]
                top = jnp.maximum(old, jnp.max(score, axis=0, keepdims=True))
                sums[0:1, cols] = top
                weights.append((jnp.exp2(score - top).astype(jnp.bfloat16), jnp.exp2(old - top)))
            for (weight, factor), cols in zip(weights, chains):
                summed = matmul(values, weight)
                sums[1:2, cols] = sums[1:2, cols] * factor + summed[HEAD : HEAD + 1]
                state[:, cols] = state[:, cols] * factor + summed[0:HEAD]

        meets = ((key_first <= a_last) & (key_last >= a_first)) | (
            (key_first <= b_last) & (key_last >= b_first)
        )
        one = (
            (key_first == key_last)
            & (a_first == key_first)
            & (a_last == key_first)
            & (b_first == key_first)
            & (b_last == key_first)
        )

        @pl.when(meets & one)
        def _():
            visit(False)

        @pl.when(meets & jnp.logical_not(one))
        def _():
            visit(True)

    if last:
        mass = sums[1:2, :]
        some = mass > 0.0
        filled = jnp.where(some, mass, 1.0)
        result = (state[...] * (1.0 / filled)).astype(jnp.bfloat16)
        logs = jnp.where(some, sums[0:1, :] + jnp.log2(filled), START)
        high = logs.astype(jnp.bfloat16).astype(jnp.float32)
        index = lax.broadcasted_iota(jnp.int32, (TAIL, columns), 0)
        tail = jnp.where(index == 0, high, logs - high).astype(jnp.bfloat16)
        for group, out in enumerate(outs):
            cols = slice(group % 2 * row_total, group % 2 * row_total + row_total)

            @pl.when(pair == group // 2)
            def _(out=out, cols=cols):
                out[0:HEAD, :] = result[:, cols]
                out[HEAD : HEAD + TAIL, :] = tail[:, cols]


def attend(info, queries, spans, blocks, state, last=False):
    first = state is None
    pairs, heads, _, columns = queries.shape
    row_total = columns // 2
    per_query = lambda rows: pl.BlockSpec((None, None, rows, columns), lambda p, h, s: (p, h, 0, 0))
    in_specs = [per_query(HEAD), pl.BlockSpec((None, 8, columns), lambda p, h, s: (p, 0, 0))]
    operands = [queries, spans]
    for arrays in blocks.values():
        in_specs += [whole(array.shape) for array in arrays]
        operands += list(arrays)
    if not first:
        in_specs += [per_query(HEAD), per_query(8)]
        operands += list(state)
    scratch = []
    if last:
        def place(pair):
            def index(p, h, s):
                return (jnp.where(p == pair, h, jnp.where(p < pair, 0, heads - 1)), 0, 0)

            return index

        out_shape = [jax.ShapeDtypeStruct((heads, HEAD + TAIL, row_total), jnp.bfloat16)] * SEQ_Y
        out_specs = [
            pl.BlockSpec((None, HEAD + TAIL, row_total), place(group // 2)) for group in range(SEQ_Y)
        ]
        scratch = [pltpu.VMEM((HEAD, columns), jnp.float32), pltpu.VMEM((8, columns), jnp.float32)]
    else:
        out_shape = [
            jax.ShapeDtypeStruct((pairs, heads, HEAD, columns), jnp.float32),
            jax.ShapeDtypeStruct((pairs, heads, 8, columns), jnp.float32),
        ]
        out_specs = [per_query(HEAD), per_query(8)]
    flops = ATTEND_FLOPS * len(blocks)
    return pl.pallas_call(
        functools.partial(attend_kernel, first, last, tuple(blocks)),
        grid_spec=pltpu.PrefetchScalarGridSpec(
            num_scalar_prefetch=1,
            grid=(pairs, heads),
            in_specs=in_specs,
            out_specs=out_specs,
            scratch_shapes=scratch,
        ),
        out_shape=out_shape,
        compiler_params=pltpu.CompilerParams(vmem_limit_bytes=48 * 2**20),
        cost_estimate=pl.CostEstimate(flops=flops, bytes_accessed=2**20, transcendentals=0),
    )(info, *operands)


def merge_kernel(*refs):
    out, parts = refs[-1], refs[:-1]
    for head in range(parts[0].shape[0]):
        logs = []
        for part in parts:
            tail = part[head, HEAD : HEAD + TAIL, :].astype(jnp.float32)
            logs.append(tail[0:1] + tail[1:2])
        top = functools.reduce(jnp.maximum, logs)
        shares = [jnp.exp2(log - top) for log in logs]
        scale = 1.0 / functools.reduce(jnp.add, shares)
        total = functools.reduce(
            jnp.add,
            [part[head, 0:HEAD, :].astype(jnp.float32) * (share * scale) for part, share in zip(parts, shares)],
        )
        out[:, head * HEAD : (head + 1) * HEAD] = total.T.astype(jnp.bfloat16)


def merge(parts):
    heads, rows, row_total = parts[0].shape
    return pl.pallas_call(
        merge_kernel,
        grid=(1,),
        in_specs=[whole(parts[0].shape)] * len(parts),
        out_specs=whole((row_total, heads * HEAD)),
        out_shape=jax.ShapeDtypeStruct((row_total, heads * HEAD), jnp.bfloat16),
        compiler_params=pltpu.CompilerParams(vmem_limit_bytes=40 * 2**20),
        cost_estimate=pl.CostEstimate(flops=10**6, bytes_accessed=2**20, transcendentals=0),
    )(*parts)


def output_kernel(where, *refs):
    out = refs[-1]
    count = (len(refs) - 1) // 2
    total = matmul(refs[0][...], refs[count][...])
    for rows, weight in zip(refs[1:count], refs[count + 1 : -1]):
        total = total + matmul(rows[...], weight[...])
    out[...] = total.astype(out.dtype)


def output(where, rows, weights, other, dtype):
    row_total, deep = rows[0].shape
    columns = weights[0].shape[1] // 2

    def side(i, where):
        return (0, 1 - where[2] if other else where[2])

    return pl.pallas_call(
        output_kernel,
        grid_spec=pltpu.PrefetchScalarGridSpec(
            num_scalar_prefetch=1,
            grid=(1,),
            in_specs=[whole((row_total, deep))] * len(rows)
            + [pl.BlockSpec((deep, columns), side)] * len(weights),
            out_specs=whole((row_total, columns)),
        ),
        out_shape=jax.ShapeDtypeStruct((row_total, columns), dtype),
        compiler_params=pltpu.CompilerParams(vmem_limit_bytes=40 * 2**20),
        cost_estimate=pl.CostEstimate(flops=3 * 10**8, bytes_accessed=2 * 2**20, transcendentals=0),
    )(where, *rows, *weights)


def per_device(
    tokens,
    query_weight,
    key_weight,
    value_weight,
    output_weight,
    adapter_down_maps,
    adapter_up_maps,
    request_lengths,
    request_adapter,
    adapter_slot,
):
    row_count = tokens.shape[0]
    col_count = query_weight.shape[1]
    slots_here = adapter_down_maps.shape[0]
    cache = lax.axis_index("cache")
    where = jnp.stack([lax.axis_index("seq"), cache, lax.axis_index("mp")]).astype(jnp.int32)
    requests = (request_lengths, request_adapter, adapter_slot)

    ups = adapter_up_maps.reshape(-1, adapter_up_maps.shape[3])
    messages = lower(where, *requests, tokens, adapter_down_maps, ups, col_count)
    messages = [messages[0]] + [lax.ppermute(messages[s], "cache", around_x(s)) for s in (1, 2, 3)]
    query, key, value, spans, info = project(
        where, request_lengths, tokens, query_weight, key_weight, value_weight
    )
    groups = [query] + [lax.ppermute(query, "seq", around_y(s)) for s in (1, 2, 3)]
    queries = jnp.stack([jnp.concatenate(groups[0:2], axis=2), jnp.concatenate(groups[2:4], axis=2)])
    packed = adapt(where, *requests, key, value, messages, slots_here)

    output_weight, _ = lax.optimization_barrier((output_weight, packed))
    chip_cols = output_weight.shape[1] // CACHE

    def columns(step):
        return lax.dynamic_slice_in_dim(output_weight, (cache + step) % CACHE * chip_cols, chip_cols, 1)

    weights = [columns(0)] + [lax.ppermute(columns(s), "cache", around_x(s)) for s in (1, 2, 3)]

    def ring(right, left):
        return lax.ppermute(right, "seq", around_z(1)), lax.ppermute(left, "seq", around_z(-1))

    half = SEQ_Z // 2
    right_1, left_1 = ring(packed, packed)
    right_2, left_2 = ring(right_1, left_1)
    near = {0: (packed,), 1: (right_1,), SEQ_Z - 1: (left_1,)}
    state = attend(info, queries, spans, near, None)
    state, right_2, left_2 = lax.optimization_barrier((state, right_2, left_2))
    right_3, left_3 = ring(right_2, left_2)
    state, *weights = lax.optimization_barrier((state, *weights))
    state = attend(info, queries, spans, {2: (right_2,), SEQ_Z - 2: (left_2,)}, state)
    state, right_3, left_3 = lax.optimization_barrier((state, right_3, left_3))
    far = ring(right_3[0], left_3[1])
    distant = {3: (right_3,), SEQ_Z - 3: (left_3,), half: far}
    parts = attend(info, queries, spans, distant, state, last=True)

    parts = [parts[0]] + [lax.ppermute(parts[g], "seq", around_y(-g)) for g in (2, 1, 3)]
    attended = merge(parts)
    rows = [attended] + [lax.ppermute(attended, "cache", around_x(s)) for s in (1, 2, 3)]
    theirs = output(where, rows, weights, True, jnp.bfloat16)
    theirs = lax.ppermute(theirs, "mp", [(0, 1), (1, 0)])
    mine = output(where, rows, weights, False, jnp.float32)
    return (mine + theirs.astype(jnp.float32)).astype(jnp.bfloat16)


def solution(mesh):
    placed = (
        P("seq", None),
        P(None, ("cache", "mp")),
        P(None, ("cache", "mp")),
        P(None, ("cache", "mp")),
        P(("cache", "mp"), None),
        P("cache", None, None),
        P("cache", None, None, None),
        P(),
        P(),
        P(),
    )
    return jax.shard_map(
        per_device, mesh=mesh, in_specs=placed, out_specs=P("seq", ("cache", "mp")), check_vma=False
    )
```

```python
import functools
import itertools
import math

import jax
import jax.numpy as jnp
from jax import lax
from jax.experimental import pallas as pl
from jax.experimental.pallas import tpu as pltpu
from jax.sharding import PartitionSpec as P

HEAD = 128
SEQ_Z = 8
SEQ_Y = 4
CACHE = 4
REQUESTS = 16
PLACES = 3
START = -1e30
NEG = -3e30
TAIL = 16
QUERY_SCALE = HEAD ** (-0.5) * math.log2(math.e)


CHUNKS = 6
ATTEND_FLOPS = 10**9


def around_z(step):
    return [
        (z * SEQ_Y + y, (z + step) % SEQ_Z * SEQ_Y + y) for z in range(SEQ_Z) for y in range(SEQ_Y)
    ]


def around_y(step):
    return [
        (z * SEQ_Y + y, z * SEQ_Y + (y + step) % SEQ_Y) for z in range(SEQ_Z) for y in range(SEQ_Y)
    ]


def around_x(step):
    return [(x, (x + step) % CACHE) for x in range(CACHE)]


def matmul(a, b, dims=((1,), (0,))):
    return lax.dot_general(a, b, (dims, ((), ())), preferred_element_type=jnp.float32)


def whole(shape):
    return pl.BlockSpec(shape, lambda *at: (0,) * len(shape))


def request_ends(known):
    bounds, at = [], jnp.int32(0)
    for r in range(REQUESTS):
        bounds.append((at, at + known[PLACES + r]))
        at = at + known[PLACES + r]
    return bounds


def slots_of_rows(places, known):
    found = jnp.zeros(places.shape, jnp.int32)
    for r, (start, _) in enumerate(request_ends(known)):
        found = jnp.where(places >= start, known[PLACES + 2 * REQUESTS + known[PLACES + REQUESTS + r]], found)
    return found


def lower_kernel(where, tokens, down, ups, *refs):
    outs, (held, maps, columns, arrived) = refs[:CACHE], refs[CACHE:]
    row_total, width = tokens.shape
    slot_total, _, low = down.shape
    up_rows = ups.shape[0]
    col_count = columns.shape[2]
    deep = width // CHUNKS
    copies = []
    for chunk in range(CHUNKS):
        part = pl.ds(chunk * deep, deep)
        copies.append(
            [pltpu.make_async_copy(tokens.at[:, part], held.at[chunk], arrived.at[chunk * 4])]
            + [
                pltpu.make_async_copy(down.at[slot, part], maps.at[chunk, slot], arrived.at[chunk * 4 + 1 + slot])
                for slot in range(slot_total)
            ]
        )
    for chunk in range(CHUNKS):
        for copy in copies[chunk]:
            copy.start()
    up_copies = []
    for step in range(CACHE):
        first = pl.multiple_of((lax.rem(where[1] + step, CACHE) * 2 + where[2]) * col_count, HEAD)
        up_copies.append(
            pltpu.make_async_copy(ups.at[:, pl.ds(first, col_count)], columns.at[step], arrived.at[CHUNKS * 4 + step])
        )
        up_copies[-1].start()
    places = where[0] * row_total + lax.broadcasted_iota(jnp.int32, (row_total, low), 0)
    mine = slots_of_rows(places, where)
    total = None
    for chunk in range(CHUNKS):
        for copy in copies[chunk]:
            copy.wait()
        pair = jnp.concatenate([maps[chunk, slot] for slot in range(slot_total)], axis=1)
        product = matmul(held[chunk], pair)
        total = product if total is None else total + product
    rows = jnp.zeros((row_total, low), jnp.float32)
    for slot in range(slot_total):
        rows = jnp.where(
            mine == where[1] * slot_total + slot, total[:, slot * low : (slot + 1) * low], rows
        )
    rows = rows.astype(jnp.bfloat16)
    for step, out in enumerate(outs):
        up_copies[step].wait()
        out[0:row_total, :] = rows
        for half in range(col_count // HEAD):
            at = row_total + half * up_rows
            out[at : at + up_rows, :] = columns[step, :, half * HEAD : (half + 1) * HEAD]


def lower(where, tokens, down, ups, col_count):
    row_total, width = tokens.shape
    slot_total, _, low = down.shape
    up_rows = ups.shape[0]
    deep = width // CHUNKS
    out_rows = row_total + up_rows * col_count // HEAD
    return pl.pallas_call(
        lower_kernel,
        grid_spec=pltpu.PrefetchScalarGridSpec(
            num_scalar_prefetch=1,
            grid=(1,),
            in_specs=[pl.BlockSpec(memory_space=pltpu.HBM)] * 3,
            out_specs=[whole((out_rows, HEAD))] * CACHE,
            scratch_shapes=[
                pltpu.VMEM((CHUNKS, row_total, deep), jnp.bfloat16),
                pltpu.VMEM((CHUNKS, slot_total, deep, low), jnp.bfloat16),
                pltpu.VMEM((CACHE, up_rows, col_count), jnp.bfloat16),
                pltpu.SemaphoreType.DMA((CHUNKS * 4 + CACHE,)),
            ],
        ),
        out_shape=[jax.ShapeDtypeStruct((out_rows, HEAD), jnp.bfloat16)] * CACHE,
        compiler_params=pltpu.CompilerParams(vmem_limit_bytes=62 * 2**20),
        cost_estimate=pl.CostEstimate(flops=6 * 10**8, bytes_accessed=6 * 2**20, transcendentals=0),
    )(where, tokens, down, ups)


def query_kernel(steps, where, tokens, wq, query, spans, info, total):
    step = pl.program_id(0)
    row_total = tokens.shape[0]
    held = tokens[...]

    @pl.when(step == 0)
    def _():
        total[...] = matmul(held, wq[...])
        bounds = request_ends(where)
        seq = where[0]
        seq_z, seq_y = lax.div(seq, SEQ_Y), lax.rem(seq, SEQ_Y)

        def request_at(row):
            found = jnp.int32(0)
            for _, end in bounds:
                found = found + (row >= end).astype(jnp.int32)
            return found

        def groups_row(group):
            return (seq_z * SEQ_Y + lax.rem(seq_y + SEQ_Y - group, SEQ_Y)) * row_total

        for group in range(SEQ_Y):
            row = groups_row(group)
            info[2 * group] = request_at(row)
            info[2 * group + 1] = request_at(row + row_total - 1)
            places = row + lax.broadcasted_iota(jnp.int32, (8, row_total), 1)
            starts = jnp.zeros(places.shape, jnp.int32)
            ends = jnp.zeros(places.shape, jnp.int32)
            for start, end in bounds:
                starts = jnp.where(places >= start, start, starts)
                ends = jnp.where(places >= start, end, ends)
            index = lax.broadcasted_iota(jnp.int32, (8, row_total), 0)
            cols = slice(group % 2 * row_total, group % 2 * row_total + row_total)
            spans[group // 2, :, cols] = jnp.where(index == 0, starts, ends)
        for back in range(SEQ_Z):
            row = (lax.rem(seq_z + SEQ_Z - back, SEQ_Z) * SEQ_Y + seq_y) * row_total
            info[8 + 3 * back] = request_at(row)
            info[8 + 3 * back + 1] = request_at(row + row_total - 1)
            info[8 + 3 * back + 2] = row

    @pl.when(step > 0)
    def _():
        total[...] += matmul(held, wq[...])

    @pl.when(step == steps - 1)
    def _():
        scaled = total[...] * QUERY_SCALE
        for head in range(query.shape[0]):
            query[head] = scaled[:, head * HEAD : (head + 1) * HEAD].T.astype(jnp.bfloat16)


def project_query(where, tokens, wq):
    steps = 3
    row_total, width = tokens.shape
    col_count = wq.shape[1]
    heads = col_count // HEAD
    deep = width // steps
    return pl.pallas_call(
        functools.partial(query_kernel, steps),
        grid_spec=pltpu.PrefetchScalarGridSpec(
            num_scalar_prefetch=1,
            grid=(steps,),
            in_specs=[
                pl.BlockSpec((row_total, deep), lambda i, *rest: (0, i)),
                pl.BlockSpec((deep, col_count), lambda i, *rest: (i, 0)),
            ],
            out_specs=[
                whole((heads, HEAD, row_total)),
                whole((SEQ_Y // 2, 8, 2 * row_total)),
                pl.BlockSpec(memory_space=pltpu.SMEM),
            ],
            scratch_shapes=[pltpu.VMEM((row_total, col_count), jnp.float32)],
        ),
        out_shape=[
            jax.ShapeDtypeStruct((heads, HEAD, row_total), jnp.bfloat16),
            jax.ShapeDtypeStruct((SEQ_Y // 2, 8, 2 * row_total), jnp.int32),
            jax.ShapeDtypeStruct((8 + 3 * SEQ_Z,), jnp.int32),
        ],
        compiler_params=pltpu.CompilerParams(vmem_limit_bytes=24 * 2**20),
        cost_estimate=pl.CostEstimate(flops=6 * 10**8, bytes_accessed=4 * 2**20, transcendentals=0),
    )(where, tokens, wq)


def project_kernel(tokens, wk, wv, key, value):
    held = tokens[...]

    @pl.when(pl.program_id(0) == 0)
    def _():
        key[...] = matmul(held, wk[...])
        value[...] = matmul(held, wv[...])

    @pl.when(pl.program_id(0) > 0)
    def _():
        key[...] += matmul(held, wk[...])
        value[...] += matmul(held, wv[...])


def project(tokens, wk, wv):
    steps = 3
    row_total, width = tokens.shape
    col_count = wk.shape[1]
    deep = width // steps
    weight = pl.BlockSpec((deep, col_count), lambda i: (i, 0))
    summed = jax.ShapeDtypeStruct((row_total, col_count), jnp.float32)
    return pl.pallas_call(
        project_kernel,
        grid=(steps,),
        in_specs=[pl.BlockSpec((row_total, deep), lambda i: (0, i)), weight, weight],
        out_specs=[whole((row_total, col_count))] * 2,
        out_shape=[summed, summed],
        compiler_params=pltpu.CompilerParams(vmem_limit_bytes=24 * 2**20),
        cost_estimate=pl.CostEstimate(flops=12 * 10**8, bytes_accessed=6 * 2**20, transcendentals=0),
    )(tokens, wk, wv)


def adapt_kernel(slot_total, where, key, value, *refs):
    messages, out = refs[:-1], refs[-1]
    row_total = key.shape[0]
    low = functools.reduce(jnp.add, [m[0:row_total, :].astype(jnp.float32) for m in messages])
    places = where[0] * row_total + lax.broadcasted_iota(jnp.int32, low.shape, 0)
    mine = slots_of_rows(places, where)
    for_key = lax.broadcasted_iota(jnp.int32, low.shape, 1) < low.shape[1] // 2
    key_low, value_low = [], []
    for step in range(len(messages)):
        for slot in range(slot_total):
            holder = lax.rem(where[1] + CACHE - step, CACHE) * slot_total + slot
            rows = jnp.where(mine == holder, low, 0.0)
            key_low.append(jnp.where(for_key, rows, 0.0).astype(jnp.bfloat16))
            value_low.append(jnp.where(for_key, 0.0, rows).astype(jnp.bfloat16))
    key_low, value_low = jnp.concatenate(key_low, axis=1), jnp.concatenate(value_low, axis=1)
    up_rows = slot_total * low.shape[1]
    for head in range(out.shape[0]):
        cols = slice(head * HEAD, (head + 1) * HEAD)
        at = row_total + head * up_rows
        up = jnp.concatenate([m[at : at + up_rows, :] for m in messages], axis=0)
        out[head, 0:row_total, :] = (key[:, cols] + matmul(key_low, up)).astype(jnp.bfloat16)
        summed = value[:, cols] + matmul(value_low, up)
        for part in range(row_total // HEAD):
            rows = slice(part * HEAD, (part + 1) * HEAD)
            out[head, row_total + part * HEAD : row_total + (part + 1) * HEAD, :] = summed[
                rows, :
            ].T.astype(jnp.bfloat16)


def adapt(where, key, value, messages, slot_total):
    row_total, col_count = key.shape
    heads = col_count // HEAD
    return pl.pallas_call(
        functools.partial(adapt_kernel, slot_total),
        grid_spec=pltpu.PrefetchScalarGridSpec(
            num_scalar_prefetch=1,
            grid=(1,),
            in_specs=[whole(a.shape) for a in (key, value, *messages)],
            out_specs=whole((heads, 2 * row_total, HEAD)),
        ),
        out_shape=jax.ShapeDtypeStruct((heads, 2 * row_total, HEAD), jnp.bfloat16),
        compiler_params=pltpu.CompilerParams(vmem_limit_bytes=32 * 2**20),
        cost_estimate=pl.CostEstimate(flops=4 * 10**8, bytes_accessed=2 * 2**20, transcendentals=0),
    )(where, key, value, *messages)


def attend_kernel(first, last, backs, info, queries, span, *refs):
    at = 0
    blocks = []
    for back in backs:
        width = 2 if back == SEQ_Z // 2 else 1
        blocks.append(refs[at : at + width])
        at += width
    if not first:
        state_in, sums_in = refs[at : at + 2]
        at += 2
    outs = refs[at:]
    state, sums = outs[-2:]
    outs = outs[:-2]
    pair, head = pl.program_id(0), pl.program_id(1)
    columns = queries.shape[1]
    row_total = columns // 2
    if first:
        state[...] = jnp.zeros(state.shape, jnp.float32)
        sums[0:1, :] = jnp.full((1, columns), START, jnp.float32)
        sums[1:2, :] = jnp.zeros((1, columns), jnp.float32)
    else:
        state[...] = state_in[...]
        sums[...] = sums_in[...]
    a_first, a_last = info[4 * pair], info[4 * pair + 1]
    b_first, b_last = info[4 * pair + 2], info[4 * pair + 3]
    index = lax.broadcasted_iota(jnp.int32, (TAIL, row_total), 0)
    ones = jnp.where(index == 0, 1.0, 0.0).astype(jnp.bfloat16)

    def meets(back):
        key_first, key_last = info[8 + 3 * back], info[8 + 3 * back + 1]
        return ((key_first <= a_last) & (key_last >= a_first)) | (
            (key_first <= b_last) & (key_last >= b_first)
        )

    def visit(chosen):
        keys, values = [], []
        for which in chosen:
            block = blocks[which]
            if len(block) == 2:
                packed = jnp.where(head == 0, block[0][...], block[1][...])
            else:
                packed = block[0][head]
            keys.append(packed[0:row_total])
            turned = [packed[at : at + HEAD] for at in range(row_total, 2 * row_total, HEAD)]
            values.append(jnp.concatenate([jnp.concatenate(turned, axis=1), ones], axis=0))
        keys, values = jnp.concatenate(keys, axis=0), jnp.concatenate(values, axis=1)
        chains = [slice(at, at + 256) for at in range(0, columns, 256)]
        scores = [matmul(keys, queries[:, cols]) for cols in chains]
        weights = []
        for score, cols in zip(scores, chains):
            masked = []
            for place, which in enumerate(chosen):
                part = score[place * row_total : (place + 1) * row_total]
                places = info[8 + 3 * backs[which] + 2] + lax.broadcasted_iota(jnp.int32, part.shape, 0)
                inside = (places >= span[0:1, cols]) & (places < span[1:2, cols])
                masked.append(jnp.where(inside, part, NEG))
            old = sums[0:1, cols]
            top = functools.reduce(
                jnp.maximum, [old] + [jnp.max(part, axis=0, keepdims=True) for part in masked]
            )
            sums[0:1, cols] = top
            parts = [jnp.exp2(part - top).astype(jnp.bfloat16) for part in masked]
            weights.append((jnp.concatenate(parts, axis=0), jnp.exp2(old - top)))
        for (weight, factor), cols in zip(weights, chains):
            summed = matmul(values, weight)
            sums[1:2, cols] = sums[1:2, cols] * factor + summed[HEAD : HEAD + 1]
            state[:, cols] = state[:, cols] * factor + summed[0:HEAD]

    needed = [meets(back) for back in backs]
    for count in range(1, len(backs) + 1):
        for chosen in itertools.combinations(range(len(backs)), count):
            only = functools.reduce(
                jnp.logical_and,
                [need if which in chosen else jnp.logical_not(need) for which, need in enumerate(needed)],
            )

            @pl.when(only)
            def _(chosen=chosen):
                visit(chosen)

    if last:
        mass = sums[1:2, :]
        some = mass > 0.0
        filled = jnp.where(some, mass, 1.0)
        result = (state[...] * (1.0 / filled)).astype(jnp.bfloat16)
        logs = jnp.where(some, sums[0:1, :] + jnp.log2(filled), START)
        high = logs.astype(jnp.bfloat16).astype(jnp.float32)
        index = lax.broadcasted_iota(jnp.int32, (TAIL, columns), 0)
        tail = jnp.where(index == 0, high, logs - high).astype(jnp.bfloat16)
        for group, out in enumerate(outs):
            cols = slice(group % 2 * row_total, group % 2 * row_total + row_total)

            @pl.when(pair == group // 2)
            def _(out=out, cols=cols):
                out[0:HEAD, :] = result[:, cols]
                out[HEAD : HEAD + TAIL, :] = tail[:, cols]


def attend(info, queries, spans, blocks, state, last=False):
    first = state is None
    pairs, heads, _, columns = queries.shape
    row_total = columns // 2
    per_query = lambda rows: pl.BlockSpec((None, None, rows, columns), lambda p, h, s: (p, h, 0, 0))
    in_specs = [per_query(HEAD), pl.BlockSpec((None, 8, columns), lambda p, h, s: (p, 0, 0))]
    operands = [queries, spans]
    for arrays in blocks.values():
        in_specs += [whole(array.shape) for array in arrays]
        operands += list(arrays)
    if not first:
        in_specs += [per_query(HEAD), per_query(8)]
        operands += list(state)
    scratch = []
    if last:
        def place(pair):
            def index(p, h, s):
                return (jnp.where(p == pair, h, jnp.where(p < pair, 0, heads - 1)), 0, 0)

            return index

        out_shape = [jax.ShapeDtypeStruct((heads, HEAD + TAIL, row_total), jnp.bfloat16)] * SEQ_Y
        out_specs = [
            pl.BlockSpec((None, HEAD + TAIL, row_total), place(group // 2)) for group in range(SEQ_Y)
        ]
        scratch = [pltpu.VMEM((HEAD, columns), jnp.float32), pltpu.VMEM((8, columns), jnp.float32)]
    else:
        out_shape = [
            jax.ShapeDtypeStruct((pairs, heads, HEAD, columns), jnp.float32),
            jax.ShapeDtypeStruct((pairs, heads, 8, columns), jnp.float32),
        ]
        out_specs = [per_query(HEAD), per_query(8)]
    flops = ATTEND_FLOPS * len(blocks)
    return pl.pallas_call(
        functools.partial(attend_kernel, first, last, tuple(blocks)),
        grid_spec=pltpu.PrefetchScalarGridSpec(
            num_scalar_prefetch=1,
            grid=(pairs, heads),
            in_specs=in_specs,
            out_specs=out_specs,
            scratch_shapes=scratch,
        ),
        out_shape=out_shape,
        compiler_params=pltpu.CompilerParams(vmem_limit_bytes=48 * 2**20),
        cost_estimate=pl.CostEstimate(flops=flops, bytes_accessed=2**20, transcendentals=0),
    )(info, *operands)


def merge_kernel(*refs):
    out, parts = refs[-1], refs[:-1]
    for head in range(parts[0].shape[0]):
        logs = []
        for part in parts:
            tail = part[head, HEAD : HEAD + TAIL, :].astype(jnp.float32)
            logs.append(tail[0:1] + tail[1:2])
        top = functools.reduce(jnp.maximum, logs)
        shares = [jnp.exp2(log - top) for log in logs]
        scale = 1.0 / functools.reduce(jnp.add, shares)
        total = functools.reduce(
            jnp.add,
            [part[head, 0:HEAD, :].astype(jnp.float32) * (share * scale) for part, share in zip(parts, shares)],
        )
        out[:, head * HEAD : (head + 1) * HEAD] = total.T.astype(jnp.bfloat16)


def merge(parts):
    heads, rows, row_total = parts[0].shape
    return pl.pallas_call(
        merge_kernel,
        grid=(1,),
        in_specs=[whole(parts[0].shape)] * len(parts),
        out_specs=whole((row_total, heads * HEAD)),
        out_shape=jax.ShapeDtypeStruct((row_total, heads * HEAD), jnp.bfloat16),
        compiler_params=pltpu.CompilerParams(vmem_limit_bytes=40 * 2**20),
        cost_estimate=pl.CostEstimate(flops=10**6, bytes_accessed=2**20, transcendentals=0),
    )(*parts)


def output_kernel(where, *refs):
    out = refs[-1]
    count = (len(refs) - 1) // 2
    total = matmul(refs[0][...], refs[count][...])
    for rows, weight in zip(refs[1:count], refs[count + 1 : -1]):
        total = total + matmul(rows[...], weight[...])
    out[...] = total.astype(out.dtype)


def output(where, rows, weights, other, dtype):
    row_total, deep = rows[0].shape
    columns = weights[0].shape[1] // 2

    def side(i, where):
        return (0, 1 - where[2] if other else where[2])

    return pl.pallas_call(
        output_kernel,
        grid_spec=pltpu.PrefetchScalarGridSpec(
            num_scalar_prefetch=1,
            grid=(1,),
            in_specs=[whole((row_total, deep))] * len(rows)
            + [pl.BlockSpec((deep, columns), side)] * len(weights),
            out_specs=whole((row_total, columns)),
        ),
        out_shape=jax.ShapeDtypeStruct((row_total, columns), dtype),
        compiler_params=pltpu.CompilerParams(vmem_limit_bytes=40 * 2**20),
        cost_estimate=pl.CostEstimate(flops=3 * 10**8, bytes_accessed=2 * 2**20, transcendentals=0),
    )(where, *rows, *weights)


def per_device(
    tokens,
    query_weight,
    key_weight,
    value_weight,
    output_weight,
    adapter_down_maps,
    adapter_up_maps,
    request_lengths,
    request_adapter,
    adapter_slot,
):
    row_count = tokens.shape[0]
    col_count = query_weight.shape[1]
    slots_here = adapter_down_maps.shape[0]
    cache = lax.axis_index("cache")
    places = jnp.stack([lax.axis_index("seq"), cache, lax.axis_index("mp")]).astype(jnp.int32)
    where = jnp.concatenate([places, request_lengths, request_adapter, adapter_slot])

    ups = adapter_up_maps.reshape(-1, adapter_up_maps.shape[3])
    messages = lower(where, tokens, adapter_down_maps, ups, col_count)
    tokens, *messages = lax.optimization_barrier((tokens, *messages))
    messages = [messages[0]] + [lax.ppermute(messages[s], "cache", around_x(s)) for s in (1, 2, 3)]
    key, value = project(tokens, key_weight, value_weight)
    tokens, key = lax.optimization_barrier((tokens, key))
    query, spans, info = project_query(where, tokens, query_weight)
    groups = [query] + [lax.ppermute(query, "seq", around_y(s)) for s in (1, 2, 3)]
    queries = jnp.stack([jnp.concatenate(groups[0:2], axis=2), jnp.concatenate(groups[2:4], axis=2)])
    packed = adapt(where, key, value, messages, slots_here)

    output_weight, _ = lax.optimization_barrier((output_weight, packed))
    chip_cols = output_weight.shape[1] // CACHE

    def columns(step):
        return lax.dynamic_slice_in_dim(output_weight, (cache + step) % CACHE * chip_cols, chip_cols, 1)

    weights = [columns(0)] + [lax.ppermute(columns(s), "cache", around_x(s)) for s in (1, 2, 3)]

    def ring(right, left):
        return lax.ppermute(right, "seq", around_z(1)), lax.ppermute(left, "seq", around_z(-1))

    half = SEQ_Z // 2
    right_1, left_1 = ring(packed, packed)
    state = attend(info, queries, spans, {0: (packed,)}, None)
    state, right_1, left_1 = lax.optimization_barrier((state, right_1, left_1))
    right_2, left_2 = ring(right_1, left_1)
    state = attend(info, queries, spans, {1: (right_1,), SEQ_Z - 1: (left_1,)}, state)
    state, right_2, left_2 = lax.optimization_barrier((state, right_2, left_2))
    right_3, left_3 = ring(right_2, left_2)
    state = attend(info, queries, spans, {2: (right_2,), SEQ_Z - 2: (left_2,)}, state)
    state, right_3, left_3 = lax.optimization_barrier((state, right_3, left_3))
    far = ring(right_3[0], left_3[1])
    state = attend(info, queries, spans, {3: (right_3,), SEQ_Z - 3: (left_3,)}, state)
    parts = attend(info, queries, spans, {half: far}, state, last=True)

    parts = [parts[0]] + [lax.ppermute(parts[g], "seq", around_y(-g)) for g in (2, 1, 3)]
    *parts, weights[1], weights[2], weights[3] = lax.optimization_barrier((*parts, *weights[1:]))
    attended = merge(parts)
    rows = [attended] + [lax.ppermute(attended, "cache", around_x(s)) for s in (1, 2, 3)]
    theirs = output(where, rows, weights, True, jnp.bfloat16)
    theirs = lax.ppermute(theirs, "mp", [(0, 1), (1, 0)])
    mine = output(where, rows, weights, False, jnp.float32)
    return (mine + theirs.astype(jnp.float32)).astype(jnp.bfloat16)


def solution(mesh):
    placed = (
        P("seq", None),
        P(None, ("cache", "mp")),
        P(None, ("cache", "mp")),
        P(None, ("cache", "mp")),
        P(("cache", "mp"), None),
        P("cache", None, None),
        P("cache", None, None, None),
        P(),
        P(),
        P(),
    )
    return jax.shard_map(
        per_device, mesh=mesh, in_specs=placed, out_specs=P("seq", ("cache", "mp")), check_vma=False
    )
```

```python
import functools
import itertools
import math

import jax
import jax.numpy as jnp
from jax import lax
from jax.experimental import pallas as pl
from jax.experimental.pallas import tpu as pltpu
from jax.sharding import PartitionSpec as P

HEAD = 128
SEQ_Z = 8
SEQ_Y = 4
CACHE = 4
REQUESTS = 16
PLACES = 3
START = -1e30
NEG = -3e30
TAIL = 16
QUERY_SCALE = HEAD ** (-0.5) * math.log2(math.e)


CHUNKS = 6
ATTEND_FLOPS = 10**6


def around_z(step):
    return [
        (z * SEQ_Y + y, (z + step) % SEQ_Z * SEQ_Y + y) for z in range(SEQ_Z) for y in range(SEQ_Y)
    ]


def around_y(step):
    return [
        (z * SEQ_Y + y, z * SEQ_Y + (y + step) % SEQ_Y) for z in range(SEQ_Z) for y in range(SEQ_Y)
    ]


def around_x(step):
    return [(x, (x + step) % CACHE) for x in range(CACHE)]


def matmul(a, b, dims=((1,), (0,))):
    return lax.dot_general(a, b, (dims, ((), ())), preferred_element_type=jnp.float32)


def whole(shape):
    return pl.BlockSpec(shape, lambda *at: (0,) * len(shape))


def request_ends(known):
    bounds, at = [], jnp.int32(0)
    for r in range(REQUESTS):
        bounds.append((at, at + known[PLACES + r]))
        at = at + known[PLACES + r]
    return bounds


def slots_of_rows(places, known):
    found = jnp.zeros(places.shape, jnp.int32)
    for r, (start, _) in enumerate(request_ends(known)):
        found = jnp.where(places >= start, known[PLACES + 2 * REQUESTS + known[PLACES + REQUESTS + r]], found)
    return found


def requests_met(where, row_total, spans, info):
    bounds = request_ends(where)
    seq = where[0]
    seq_z, seq_y = lax.div(seq, SEQ_Y), lax.rem(seq, SEQ_Y)

    def request_at(row):
        found = jnp.int32(0)
        for _, end in bounds:
            found = found + (row >= end).astype(jnp.int32)
        return found

    def groups_row(group):
        return (seq_z * SEQ_Y + lax.rem(seq_y + SEQ_Y - group, SEQ_Y)) * row_total

    for group in range(SEQ_Y):
        row = groups_row(group)
        info[2 * group] = request_at(row)
        info[2 * group + 1] = request_at(row + row_total - 1)
        places = row + lax.broadcasted_iota(jnp.int32, (8, row_total), 1)
        starts = jnp.zeros(places.shape, jnp.int32)
        ends = jnp.zeros(places.shape, jnp.int32)
        for start, end in bounds:
            starts = jnp.where(places >= start, start, starts)
            ends = jnp.where(places >= start, end, ends)
        index = lax.broadcasted_iota(jnp.int32, (8, row_total), 0)
        cols = slice(group % 2 * row_total, group % 2 * row_total + row_total)
        spans[group // 2, :, cols] = jnp.where(index == 0, starts, ends)
    for back in range(SEQ_Z):
        row = (lax.rem(seq_z + SEQ_Z - back, SEQ_Z) * SEQ_Y + seq_y) * row_total
        info[8 + 3 * back] = request_at(row)
        info[8 + 3 * back + 1] = request_at(row + row_total - 1)
        info[8 + 3 * back + 2] = row


def lower_kernel(where, tokens, down, ups, *refs):
    outs, (spans, info, held, maps, columns, arrived) = refs[:CACHE], refs[CACHE:]
    row_total, width = tokens.shape
    slot_total, _, low = down.shape
    up_rows = ups.shape[0]
    col_count = columns.shape[2]
    deep = width // CHUNKS
    copies = []
    for chunk in range(CHUNKS):
        part = pl.ds(chunk * deep, deep)
        copies.append(
            [pltpu.make_async_copy(tokens.at[:, part], held.at[chunk], arrived.at[chunk * 4])]
            + [
                pltpu.make_async_copy(down.at[slot, part], maps.at[chunk, slot], arrived.at[chunk * 4 + 1 + slot])
                for slot in range(slot_total)
            ]
        )
    for chunk in range(CHUNKS):
        for copy in copies[chunk]:
            copy.start()
    up_copies = []
    for step in range(CACHE):
        first = pl.multiple_of((lax.rem(where[1] + step, CACHE) * 2 + where[2]) * col_count, HEAD)
        up_copies.append(
            pltpu.make_async_copy(ups.at[:, pl.ds(first, col_count)], columns.at[step], arrived.at[CHUNKS * 4 + step])
        )
        up_copies[-1].start()
    requests_met(where, row_total, spans, info)
    places = where[0] * row_total + lax.broadcasted_iota(jnp.int32, (row_total, low), 0)
    mine = slots_of_rows(places, where)
    total = None
    for chunk in range(CHUNKS):
        for copy in copies[chunk]:
            copy.wait()
        pair = jnp.concatenate([maps[chunk, slot] for slot in range(slot_total)], axis=1)
        product = matmul(held[chunk], pair)
        total = product if total is None else total + product
    rows = jnp.zeros((row_total, low), jnp.float32)
    for slot in range(slot_total):
        rows = jnp.where(
            mine == where[1] * slot_total + slot, total[:, slot * low : (slot + 1) * low], rows
        )
    rows = rows.astype(jnp.bfloat16)
    for step, out in enumerate(outs):
        up_copies[step].wait()
        out[0:row_total, :] = rows
        for half in range(col_count // HEAD):
            at = row_total + half * up_rows
            out[at : at + up_rows, :] = columns[step, :, half * HEAD : (half + 1) * HEAD]


def lower(where, tokens, down, ups, col_count):
    row_total, width = tokens.shape
    slot_total, _, low = down.shape
    up_rows = ups.shape[0]
    deep = width // CHUNKS
    out_rows = row_total + up_rows * col_count // HEAD
    return pl.pallas_call(
        lower_kernel,
        grid_spec=pltpu.PrefetchScalarGridSpec(
            num_scalar_prefetch=1,
            grid=(1,),
            in_specs=[pl.BlockSpec(memory_space=pltpu.HBM)] * 3,
            out_specs=[whole((out_rows, HEAD))] * CACHE
            + [whole((SEQ_Y // 2, 8, 2 * row_total)), pl.BlockSpec(memory_space=pltpu.SMEM)],
            scratch_shapes=[
                pltpu.VMEM((CHUNKS, row_total, deep), jnp.bfloat16),
                pltpu.VMEM((CHUNKS, slot_total, deep, low), jnp.bfloat16),
                pltpu.VMEM((CACHE, up_rows, col_count), jnp.bfloat16),
                pltpu.SemaphoreType.DMA((CHUNKS * 4 + CACHE,)),
            ],
        ),
        out_shape=[jax.ShapeDtypeStruct((out_rows, HEAD), jnp.bfloat16)] * CACHE
        + [
            jax.ShapeDtypeStruct((SEQ_Y // 2, 8, 2 * row_total), jnp.int32),
            jax.ShapeDtypeStruct((8 + 3 * SEQ_Z,), jnp.int32),
        ],
        compiler_params=pltpu.CompilerParams(vmem_limit_bytes=62 * 2**20),
        cost_estimate=pl.CostEstimate(flops=6 * 10**8, bytes_accessed=6 * 2**20, transcendentals=0),
    )(where, tokens, down, ups)


def query_kernel(steps, tokens, wq, query, total):
    step = pl.program_id(0)
    row_total = tokens.shape[0]
    held = tokens[...]

    @pl.when(step == 0)
    def _():
        total[...] = matmul(held, wq[...])

    @pl.when(step > 0)
    def _():
        total[...] += matmul(held, wq[...])

    @pl.when(step == steps - 1)
    def _():
        scaled = total[...] * QUERY_SCALE
        for head in range(query.shape[0]):
            query[head] = scaled[:, head * HEAD : (head + 1) * HEAD].T.astype(jnp.bfloat16)


def project_query(tokens, wq):
    steps = 3
    row_total, width = tokens.shape
    col_count = wq.shape[1]
    heads = col_count // HEAD
    deep = width // steps
    return pl.pallas_call(
        functools.partial(query_kernel, steps),
        grid=(steps,),
        in_specs=[
            pl.BlockSpec((row_total, deep), lambda i: (0, i)),
            pl.BlockSpec((deep, col_count), lambda i: (i, 0)),
        ],
        out_specs=whole((heads, HEAD, row_total)),
        scratch_shapes=[pltpu.VMEM((row_total, col_count), jnp.float32)],
        out_shape=jax.ShapeDtypeStruct((heads, HEAD, row_total), jnp.bfloat16),
        compiler_params=pltpu.CompilerParams(vmem_limit_bytes=24 * 2**20),
        cost_estimate=pl.CostEstimate(flops=6 * 10**8, bytes_accessed=4 * 2**20, transcendentals=0),
    )(tokens, wq)


def project_kernel(tokens, wk, wv, key, value):
    held = tokens[...]

    @pl.when(pl.program_id(0) == 0)
    def _():
        key[...] = matmul(held, wk[...])
        value[...] = matmul(held, wv[...])

    @pl.when(pl.program_id(0) > 0)
    def _():
        key[...] += matmul(held, wk[...])
        value[...] += matmul(held, wv[...])


def project(tokens, wk, wv):
    steps = 3
    row_total, width = tokens.shape
    col_count = wk.shape[1]
    deep = width // steps
    weight = pl.BlockSpec((deep, col_count), lambda i: (i, 0))
    summed = jax.ShapeDtypeStruct((row_total, col_count), jnp.float32)
    return pl.pallas_call(
        project_kernel,
        grid=(steps,),
        in_specs=[pl.BlockSpec((row_total, deep), lambda i: (0, i)), weight, weight],
        out_specs=[whole((row_total, col_count))] * 2,
        out_shape=[summed, summed],
        compiler_params=pltpu.CompilerParams(vmem_limit_bytes=24 * 2**20),
        cost_estimate=pl.CostEstimate(flops=12 * 10**8, bytes_accessed=6 * 2**20, transcendentals=0),
    )(tokens, wk, wv)


def adapt_kernel(slot_total, where, key, value, *refs):
    messages, out = refs[:-1], refs[-1]
    row_total = key.shape[0]
    low = functools.reduce(jnp.add, [m[0:row_total, :].astype(jnp.float32) for m in messages])
    places = where[0] * row_total + lax.broadcasted_iota(jnp.int32, low.shape, 0)
    mine = slots_of_rows(places, where)
    for_key = lax.broadcasted_iota(jnp.int32, low.shape, 1) < low.shape[1] // 2
    key_low, value_low = [], []
    for step in range(len(messages)):
        for slot in range(slot_total):
            holder = lax.rem(where[1] + CACHE - step, CACHE) * slot_total + slot
            rows = jnp.where(mine == holder, low, 0.0)
            key_low.append(jnp.where(for_key, rows, 0.0).astype(jnp.bfloat16))
            value_low.append(jnp.where(for_key, 0.0, rows).astype(jnp.bfloat16))
    key_low, value_low = jnp.concatenate(key_low, axis=1), jnp.concatenate(value_low, axis=1)
    up_rows = slot_total * low.shape[1]
    for head in range(out.shape[0]):
        cols = slice(head * HEAD, (head + 1) * HEAD)
        at = row_total + head * up_rows
        up = jnp.concatenate([m[at : at + up_rows, :] for m in messages], axis=0)
        out[head, 0:row_total, :] = (key[:, cols] + matmul(key_low, up)).astype(jnp.bfloat16)
        summed = value[:, cols] + matmul(value_low, up)
        for part in range(row_total // HEAD):
            rows = slice(part * HEAD, (part + 1) * HEAD)
            out[head, row_total + part * HEAD : row_total + (part + 1) * HEAD, :] = summed[
                rows, :
            ].T.astype(jnp.bfloat16)


def adapt(where, key, value, messages, slot_total):
    row_total, col_count = key.shape
    heads = col_count // HEAD
    return pl.pallas_call(
        functools.partial(adapt_kernel, slot_total),
        grid_spec=pltpu.PrefetchScalarGridSpec(
            num_scalar_prefetch=1,
            grid=(1,),
            in_specs=[whole(a.shape) for a in (key, value, *messages)],
            out_specs=whole((heads, 2 * row_total, HEAD)),
        ),
        out_shape=jax.ShapeDtypeStruct((heads, 2 * row_total, HEAD), jnp.bfloat16),
        compiler_params=pltpu.CompilerParams(vmem_limit_bytes=32 * 2**20),
        cost_estimate=pl.CostEstimate(flops=4 * 10**8, bytes_accessed=2 * 2**20, transcendentals=0),
    )(where, key, value, *messages)


def attend_kernel(first, last, backs, info, queries, span, *refs):
    at = 0
    blocks = []
    for back in backs:
        width = 2 if back == SEQ_Z // 2 else 1
        blocks.append(refs[at : at + width])
        at += width
    if not first:
        state_in, sums_in = refs[at : at + 2]
        at += 2
    outs = refs[at:]
    state, sums = outs[-2:]
    outs = outs[:-2]
    pair, head = pl.program_id(0), pl.program_id(1)
    columns = queries.shape[1]
    row_total = columns // 2
    if first:
        state[...] = jnp.zeros(state.shape, jnp.float32)
        sums[0:1, :] = jnp.full((1, columns), START, jnp.float32)
        sums[1:2, :] = jnp.zeros((1, columns), jnp.float32)
    else:
        state[...] = state_in[...]
        sums[...] = sums_in[...]
    a_first, a_last = info[4 * pair], info[4 * pair + 1]
    b_first, b_last = info[4 * pair + 2], info[4 * pair + 3]
    index = lax.broadcasted_iota(jnp.int32, (TAIL, row_total), 0)
    ones = jnp.where(index == 0, 1.0, 0.0).astype(jnp.bfloat16)

    def meets(back):
        key_first, key_last = info[8 + 3 * back], info[8 + 3 * back + 1]
        return ((key_first <= a_last) & (key_last >= a_first)) | (
            (key_first <= b_last) & (key_last >= b_first)
        )

    def visit(chosen):
        keys, values = [], []
        for which in chosen:
            block = blocks[which]
            if len(block) == 2:
                packed = jnp.where(head == 0, block[0][...], block[1][...])
            else:
                packed = block[0][head]
            keys.append(packed[0:row_total])
            turned = [packed[at : at + HEAD] for at in range(row_total, 2 * row_total, HEAD)]
            values.append(jnp.concatenate([jnp.concatenate(turned, axis=1), ones], axis=0))
        keys, values = jnp.concatenate(keys, axis=0), jnp.concatenate(values, axis=1)
        chains = [slice(at, at + 256) for at in range(0, columns, 256)]
        scores = [matmul(keys, queries[:, cols]) for cols in chains]
        weights = []
        for score, cols in zip(scores, chains):
            masked = []
            for place, which in enumerate(chosen):
                part = score[place * row_total : (place + 1) * row_total]
                places = info[8 + 3 * backs[which] + 2] + lax.broadcasted_iota(jnp.int32, part.shape, 0)
                inside = (places >= span[0:1, cols]) & (places < span[1:2, cols])
                masked.append(jnp.where(inside, part, NEG))
            old = sums[0:1, cols]
            top = functools.reduce(
                jnp.maximum, [old] + [jnp.max(part, axis=0, keepdims=True) for part in masked]
            )
            sums[0:1, cols] = top
            parts = [jnp.exp2(part - top).astype(jnp.bfloat16) for part in masked]
            weights.append((jnp.concatenate(parts, axis=0), jnp.exp2(old - top)))
        for (weight, factor), cols in zip(weights, chains):
            summed = matmul(values, weight)
            sums[1:2, cols] = sums[1:2, cols] * factor + summed[HEAD : HEAD + 1]
            state[:, cols] = state[:, cols] * factor + summed[0:HEAD]

    needed = [meets(back) for back in backs]
    for count in range(1, len(backs) + 1):
        for chosen in itertools.combinations(range(len(backs)), count):
            only = functools.reduce(
                jnp.logical_and,
                [need if which in chosen else jnp.logical_not(need) for which, need in enumerate(needed)],
            )

            @pl.when(only)
            def _(chosen=chosen):
                visit(chosen)

    if last:
        mass = sums[1:2, :]
        some = mass > 0.0
        filled = jnp.where(some, mass, 1.0)
        result = (state[...] * (1.0 / filled)).astype(jnp.bfloat16)
        logs = jnp.where(some, sums[0:1, :] + jnp.log2(filled), START)
        high = logs.astype(jnp.bfloat16).astype(jnp.float32)
        index = lax.broadcasted_iota(jnp.int32, (TAIL, columns), 0)
        tail = jnp.where(index == 0, high, logs - high).astype(jnp.bfloat16)
        for group, out in enumerate(outs):
            cols = slice(group % 2 * row_total, group % 2 * row_total + row_total)

            @pl.when(pair == group // 2)
            def _(out=out, cols=cols):
                out[0:HEAD, :] = result[:, cols]
                out[HEAD : HEAD + TAIL, :] = tail[:, cols]


def attend(info, queries, spans, blocks, state, last=False):
    first = state is None
    pairs, heads, _, columns = queries.shape
    row_total = columns // 2
    per_query = lambda rows: pl.BlockSpec((None, None, rows, columns), lambda p, h, s: (p, h, 0, 0))
    in_specs = [per_query(HEAD), pl.BlockSpec((None, 8, columns), lambda p, h, s: (p, 0, 0))]
    operands = [queries, spans]
    for arrays in blocks.values():
        in_specs += [whole(array.shape) for array in arrays]
        operands += list(arrays)
    if not first:
        in_specs += [per_query(HEAD), per_query(8)]
        operands += list(state)
    scratch = []
    if last:
        def place(pair):
            def index(p, h, s):
                return (jnp.where(p == pair, h, jnp.where(p < pair, 0, heads - 1)), 0, 0)

            return index

        out_shape = [jax.ShapeDtypeStruct((heads, HEAD + TAIL, row_total), jnp.bfloat16)] * SEQ_Y
        out_specs = [
            pl.BlockSpec((None, HEAD + TAIL, row_total), place(group // 2)) for group in range(SEQ_Y)
        ]
        scratch = [pltpu.VMEM((HEAD, columns), jnp.float32), pltpu.VMEM((8, columns), jnp.float32)]
    else:
        out_shape = [
            jax.ShapeDtypeStruct((pairs, heads, HEAD, columns), jnp.float32),
            jax.ShapeDtypeStruct((pairs, heads, 8, columns), jnp.float32),
        ]
        out_specs = [per_query(HEAD), per_query(8)]
    flops = ATTEND_FLOPS * len(blocks)
    return pl.pallas_call(
        functools.partial(attend_kernel, first, last, tuple(blocks)),
        grid_spec=pltpu.PrefetchScalarGridSpec(
            num_scalar_prefetch=1,
            grid=(pairs, heads),
            in_specs=in_specs,
            out_specs=out_specs,
            scratch_shapes=scratch,
        ),
        out_shape=out_shape,
        compiler_params=pltpu.CompilerParams(vmem_limit_bytes=24 * 2**20),
        cost_estimate=pl.CostEstimate(flops=flops, bytes_accessed=2**20, transcendentals=0),
    )(info, *operands)


def merge_kernel(*refs):
    out, parts = refs[-1], refs[:-1]
    for head in range(parts[0].shape[0]):
        logs = []
        for part in parts:
            tail = part[head, HEAD : HEAD + TAIL, :].astype(jnp.float32)
            logs.append(tail[0:1] + tail[1:2])
        top = functools.reduce(jnp.maximum, logs)
        shares = [jnp.exp2(log - top) for log in logs]
        scale = 1.0 / functools.reduce(jnp.add, shares)
        total = functools.reduce(
            jnp.add,
            [part[head, 0:HEAD, :].astype(jnp.float32) * (share * scale) for part, share in zip(parts, shares)],
        )
        out[:, head * HEAD : (head + 1) * HEAD] = total.T.astype(jnp.bfloat16)


def merge(parts):
    heads, rows, row_total = parts[0].shape
    return pl.pallas_call(
        merge_kernel,
        grid=(1,),
        in_specs=[whole(parts[0].shape)] * len(parts),
        out_specs=whole((row_total, heads * HEAD)),
        out_shape=jax.ShapeDtypeStruct((row_total, heads * HEAD), jnp.bfloat16),
        compiler_params=pltpu.CompilerParams(vmem_limit_bytes=40 * 2**20),
        cost_estimate=pl.CostEstimate(flops=10**6, bytes_accessed=2**20, transcendentals=0),
    )(*parts)


def output_kernel(where, *refs):
    out = refs[-1]
    count = (len(refs) - 1) // 2
    total = matmul(refs[0][...], refs[count][...])
    for rows, weight in zip(refs[1:count], refs[count + 1 : -1]):
        total = total + matmul(rows[...], weight[...])
    out[...] = total.astype(out.dtype)


def output(where, rows, weights, other, dtype):
    row_total, deep = rows[0].shape
    columns = weights[0].shape[1] // 2

    def side(i, where):
        return (0, 1 - where[2] if other else where[2])

    return pl.pallas_call(
        output_kernel,
        grid_spec=pltpu.PrefetchScalarGridSpec(
            num_scalar_prefetch=1,
            grid=(1,),
            in_specs=[whole((row_total, deep))] * len(rows)
            + [pl.BlockSpec((deep, columns), side)] * len(weights),
            out_specs=whole((row_total, columns)),
        ),
        out_shape=jax.ShapeDtypeStruct((row_total, columns), dtype),
        compiler_params=pltpu.CompilerParams(vmem_limit_bytes=40 * 2**20),
        cost_estimate=pl.CostEstimate(flops=3 * 10**8, bytes_accessed=2 * 2**20, transcendentals=0),
    )(where, *rows, *weights)


def per_device(
    tokens,
    query_weight,
    key_weight,
    value_weight,
    output_weight,
    adapter_down_maps,
    adapter_up_maps,
    request_lengths,
    request_adapter,
    adapter_slot,
):
    row_count = tokens.shape[0]
    col_count = query_weight.shape[1]
    slots_here = adapter_down_maps.shape[0]
    cache = lax.axis_index("cache")
    known = [jnp.stack([lax.axis_index("seq"), cache, lax.axis_index("mp")]).astype(jnp.int32)]
    known += [request_lengths, request_adapter, adapter_slot]
    known_total = sum(array.shape[0] for array in known)
    where, at = jnp.zeros((known_total,), jnp.int32), 0
    for array in known:
        where = where + jnp.pad(array, (at, known_total - at - array.shape[0]))
        at = at + array.shape[0]

    ups = adapter_up_maps.reshape(-1, adapter_up_maps.shape[3])
    *messages, spans, info = lower(where, tokens, adapter_down_maps, ups, col_count)
    tokens, *messages = lax.optimization_barrier((tokens, *messages))
    messages = [messages[0]] + [lax.ppermute(messages[s], "cache", around_x(s)) for s in (1, 2, 3)]
    key, value = project(tokens, key_weight, value_weight)
    tokens, key = lax.optimization_barrier((tokens, key))
    query = project_query(tokens, query_weight)
    groups = [query] + [lax.ppermute(query, "seq", around_y(s)) for s in (1, 2, 3)]
    queries = jnp.stack([jnp.concatenate(groups[0:2], axis=2), jnp.concatenate(groups[2:4], axis=2)])
    packed = adapt(where, key, value, messages, slots_here)

    output_weight, _ = lax.optimization_barrier((output_weight, packed))
    chip_cols = output_weight.shape[1] // CACHE

    def columns(step):
        return lax.dynamic_slice_in_dim(output_weight, (cache + step) % CACHE * chip_cols, chip_cols, 1)

    weights = [columns(0)] + [lax.ppermute(columns(s), "cache", around_x(s)) for s in (1, 2, 3)]

    def ring(right, left):
        return lax.ppermute(right, "seq", around_z(1)), lax.ppermute(left, "seq", around_z(-1))

    half = SEQ_Z // 2
    right_1, left_1 = ring(packed, packed)
    state = attend(info, queries, spans, {0: (packed,)}, None)
    right_1 = lax.optimization_barrier((state[0], right_1))[1]
    left_1 = lax.optimization_barrier((state[0], left_1))[1]
    right_2, left_2 = ring(right_1, left_1)
    state = attend(info, queries, spans, {1: (right_1,), SEQ_Z - 1: (left_1,)}, state)
    right_2 = lax.optimization_barrier((state[0], right_2))[1]
    left_2 = lax.optimization_barrier((state[0], left_2))[1]
    right_3, left_3 = ring(right_2, left_2)
    state, weights[1] = lax.optimization_barrier((state, weights[1]))
    state = attend(info, queries, spans, {2: (right_2,), SEQ_Z - 2: (left_2,)}, state)
    right_3 = lax.optimization_barrier((state[0], right_3))[1]
    left_3 = lax.optimization_barrier((state[0], left_3))[1]
    far = ring(right_3[0], left_3[1])
    state, weights[3] = lax.optimization_barrier((state, weights[3]))
    state = attend(info, queries, spans, {3: (right_3,), SEQ_Z - 3: (left_3,)}, state)
    parts = attend(info, queries, spans, {half: far}, state, last=True)

    parts = [parts[0]] + [lax.ppermute(parts[g], "seq", around_y(-g)) for g in (2, 1, 3)]
    *parts, weights[2] = lax.optimization_barrier((*parts, weights[2]))
    attended = merge(parts)
    rows = [attended] + [lax.ppermute(attended, "cache", around_x(s)) for s in (1, 2, 3)]
    theirs = output(where, rows, weights, True, jnp.bfloat16)
    theirs = lax.ppermute(theirs, "mp", [(0, 1), (1, 0)])
    mine = output(where, rows, weights, False, jnp.float32)
    return (mine + theirs.astype(jnp.float32)).astype(jnp.bfloat16)


def solution(mesh):
    placed = (
        P("seq", None),
        P(None, ("cache", "mp")),
        P(None, ("cache", "mp")),
        P(None, ("cache", "mp")),
        P(("cache", "mp"), None),
        P("cache", None, None),
        P("cache", None, None, None),
        P(),
        P(),
        P(),
    )
    return jax.shard_map(
        per_device, mesh=mesh, in_specs=placed, out_specs=P("seq", ("cache", "mp")), check_vma=False
    )
```

```python
import functools
import itertools
import math

import jax
import jax.numpy as jnp
from jax import lax
from jax.experimental import pallas as pl
from jax.experimental.pallas import tpu as pltpu
from jax.sharding import PartitionSpec as P

HEAD = 128
SEQ_Z = 8
SEQ_Y = 4
CACHE = 4
REQUESTS = 16
PLACES = 3
START = -1e30
NEG = -3e30
TAIL = 16
QUERY_SCALE = HEAD ** (-0.5) * math.log2(math.e)


CHUNKS = 2
ATTEND_FLOPS = 10**6


def around_z(step):
    return [
        (z * SEQ_Y + y, (z + step) % SEQ_Z * SEQ_Y + y) for z in range(SEQ_Z) for y in range(SEQ_Y)
    ]


def around_y(step):
    return [
        (z * SEQ_Y + y, z * SEQ_Y + (y + step) % SEQ_Y) for z in range(SEQ_Z) for y in range(SEQ_Y)
    ]


def around_x(step):
    return [(x, (x + step) % CACHE) for x in range(CACHE)]


def matmul(a, b, dims=((1,), (0,))):
    return lax.dot_general(a, b, (dims, ((), ())), preferred_element_type=jnp.float32)


def whole(shape):
    return pl.BlockSpec(shape, lambda *at: (0,) * len(shape))


def request_ends(known):
    bounds, at = [], jnp.int32(0)
    for r in range(REQUESTS):
        bounds.append((at, at + known[PLACES + r]))
        at = at + known[PLACES + r]
    return bounds


def slots_of_rows(places, known):
    found = jnp.zeros(places.shape, jnp.int32)
    for r, (start, _) in enumerate(request_ends(known)):
        found = jnp.where(places >= start, known[PLACES + 2 * REQUESTS + known[PLACES + REQUESTS + r]], found)
    return found


def requests_met(where, row_total, spans, info):
    bounds = request_ends(where)
    seq = where[0]
    seq_z, seq_y = lax.div(seq, SEQ_Y), lax.rem(seq, SEQ_Y)

    def request_at(row):
        found = jnp.int32(0)
        for _, end in bounds:
            found = found + (row >= end).astype(jnp.int32)
        return found

    def groups_row(group):
        return (seq_z * SEQ_Y + lax.rem(seq_y + SEQ_Y - group, SEQ_Y)) * row_total

    for group in range(SEQ_Y):
        row = groups_row(group)
        info[2 * group] = request_at(row)
        info[2 * group + 1] = request_at(row + row_total - 1)
        places = row + lax.broadcasted_iota(jnp.int32, (8, row_total), 1)
        starts = jnp.zeros(places.shape, jnp.int32)
        ends = jnp.zeros(places.shape, jnp.int32)
        for start, end in bounds:
            starts = jnp.where(places >= start, start, starts)
            ends = jnp.where(places >= start, end, ends)
        index = lax.broadcasted_iota(jnp.int32, (8, row_total), 0)
        cols = slice(group % 2 * row_total, group % 2 * row_total + row_total)
        spans[group // 2, :, cols] = jnp.where(index == 0, starts, ends)
    for back in range(SEQ_Z):
        row = (lax.rem(seq_z + SEQ_Z - back, SEQ_Z) * SEQ_Y + seq_y) * row_total
        info[8 + 3 * back] = request_at(row)
        info[8 + 3 * back + 1] = request_at(row + row_total - 1)
        info[8 + 3 * back + 2] = row


def lower_kernel(where, tokens, down, ups, *refs):
    outs, (spans, info, held, maps, columns, arrived) = refs[:CACHE], refs[CACHE:]
    row_total, width = tokens.shape
    slot_total, _, low = down.shape
    up_rows = ups.shape[0]
    col_count = columns.shape[2]
    deep = width // CHUNKS
    copies = []
    for chunk in range(CHUNKS):
        part = pl.ds(chunk * deep, deep)
        copies.append(
            [pltpu.make_async_copy(tokens.at[:, part], held.at[chunk], arrived.at[chunk * 4])]
            + [
                pltpu.make_async_copy(down.at[slot, part], maps.at[chunk, slot], arrived.at[chunk * 4 + 1 + slot])
                for slot in range(slot_total)
            ]
        )
    for chunk in range(CHUNKS):
        for copy in copies[chunk]:
            copy.start()
    up_copies = []
    for step in range(CACHE):
        first = pl.multiple_of((lax.rem(where[1] + step, CACHE) * 2 + where[2]) * col_count, HEAD)
        up_copies.append(
            pltpu.make_async_copy(ups.at[:, pl.ds(first, col_count)], columns.at[step], arrived.at[CHUNKS * 4 + step])
        )
        up_copies[-1].start()
    requests_met(where, row_total, spans, info)
    places = where[0] * row_total + lax.broadcasted_iota(jnp.int32, (row_total, low), 0)
    mine = slots_of_rows(places, where)
    total = None
    for chunk in range(CHUNKS):
        for copy in copies[chunk]:
            copy.wait()
        pair = jnp.concatenate([maps[chunk, slot] for slot in range(slot_total)], axis=1)
        product = matmul(held[chunk], pair)
        total = product if total is None else total + product
    rows = jnp.zeros((row_total, low), jnp.float32)
    for slot in range(slot_total):
        rows = jnp.where(
            mine == where[1] * slot_total + slot, total[:, slot * low : (slot + 1) * low], rows
        )
    rows = rows.astype(jnp.bfloat16)
    for step, out in enumerate(outs):
        up_copies[step].wait()
        out[0:row_total, :] = rows
        for half in range(col_count // HEAD):
            at = row_total + half * up_rows
            out[at : at + up_rows, :] = columns[step, :, half * HEAD : (half + 1) * HEAD]


def lower(where, tokens, down, ups, col_count):
    row_total, width = tokens.shape
    slot_total, _, low = down.shape
    up_rows = ups.shape[0]
    deep = width // CHUNKS
    out_rows = row_total + up_rows * col_count // HEAD
    return pl.pallas_call(
        lower_kernel,
        grid_spec=pltpu.PrefetchScalarGridSpec(
            num_scalar_prefetch=1,
            grid=(1,),
            in_specs=[pl.BlockSpec(memory_space=pltpu.HBM)] * 3,
            out_specs=[whole((out_rows, HEAD))] * CACHE
            + [whole((SEQ_Y // 2, 8, 2 * row_total)), pl.BlockSpec(memory_space=pltpu.SMEM)],
            scratch_shapes=[
                pltpu.VMEM((CHUNKS, row_total, deep), jnp.bfloat16),
                pltpu.VMEM((CHUNKS, slot_total, deep, low), jnp.bfloat16),
                pltpu.VMEM((CACHE, up_rows, col_count), jnp.bfloat16),
                pltpu.SemaphoreType.DMA((CHUNKS * 4 + CACHE,)),
            ],
        ),
        out_shape=[jax.ShapeDtypeStruct((out_rows, HEAD), jnp.bfloat16)] * CACHE
        + [
            jax.ShapeDtypeStruct((SEQ_Y // 2, 8, 2 * row_total), jnp.int32),
            jax.ShapeDtypeStruct((8 + 3 * SEQ_Z,), jnp.int32),
        ],
        compiler_params=pltpu.CompilerParams(vmem_limit_bytes=62 * 2**20),
        cost_estimate=pl.CostEstimate(flops=6 * 10**8, bytes_accessed=6 * 2**20, transcendentals=0),
    )(where, tokens, down, ups)


def query_kernel(steps, tokens, wq, query, total):
    step = pl.program_id(0)
    row_total = tokens.shape[0]
    held = tokens[...]

    @pl.when(step == 0)
    def _():
        total[...] = matmul(held, wq[...])

    @pl.when(step > 0)
    def _():
        total[...] += matmul(held, wq[...])

    @pl.when(step == steps - 1)
    def _():
        scaled = total[...] * QUERY_SCALE
        for head in range(query.shape[0]):
            query[head] = scaled[:, head * HEAD : (head + 1) * HEAD].T.astype(jnp.bfloat16)


def project_query(tokens, wq):
    steps = 3
    row_total, width = tokens.shape
    col_count = wq.shape[1]
    heads = col_count // HEAD
    deep = width // steps
    return pl.pallas_call(
        functools.partial(query_kernel, steps),
        grid=(steps,),
        in_specs=[
            pl.BlockSpec((row_total, deep), lambda i: (0, i)),
            pl.BlockSpec((deep, col_count), lambda i: (i, 0)),
        ],
        out_specs=whole((heads, HEAD, row_total)),
        scratch_shapes=[pltpu.VMEM((row_total, col_count), jnp.float32)],
        out_shape=jax.ShapeDtypeStruct((heads, HEAD, row_total), jnp.bfloat16),
        compiler_params=pltpu.CompilerParams(vmem_limit_bytes=24 * 2**20),
        cost_estimate=pl.CostEstimate(flops=6 * 10**8, bytes_accessed=4 * 2**20, transcendentals=0),
    )(tokens, wq)


def project_kernel(tokens, wk, wv, key, value):
    held = tokens[...]

    @pl.when(pl.program_id(0) == 0)
    def _():
        key[...] = matmul(held, wk[...])
        value[...] = matmul(held, wv[...])

    @pl.when(pl.program_id(0) > 0)
    def _():
        key[...] += matmul(held, wk[...])
        value[...] += matmul(held, wv[...])


def project(tokens, wk, wv):
    steps = 3
    row_total, width = tokens.shape
    col_count = wk.shape[1]
    deep = width // steps
    weight = pl.BlockSpec((deep, col_count), lambda i: (i, 0))
    summed = jax.ShapeDtypeStruct((row_total, col_count), jnp.float32)
    return pl.pallas_call(
        project_kernel,
        grid=(steps,),
        in_specs=[pl.BlockSpec((row_total, deep), lambda i: (0, i)), weight, weight],
        out_specs=[whole((row_total, col_count))] * 2,
        out_shape=[summed, summed],
        compiler_params=pltpu.CompilerParams(vmem_limit_bytes=24 * 2**20),
        cost_estimate=pl.CostEstimate(flops=12 * 10**8, bytes_accessed=6 * 2**20, transcendentals=0),
    )(tokens, wk, wv)


def adapt_kernel(slot_total, where, key, value, *refs):
    messages, out = refs[:-1], refs[-1]
    row_total = key.shape[0]
    low = functools.reduce(jnp.add, [m[0:row_total, :].astype(jnp.float32) for m in messages])
    places = where[0] * row_total + lax.broadcasted_iota(jnp.int32, low.shape, 0)
    mine = slots_of_rows(places, where)
    for_key = lax.broadcasted_iota(jnp.int32, low.shape, 1) < low.shape[1] // 2
    key_low, value_low = [], []
    for step in range(len(messages)):
        for slot in range(slot_total):
            holder = lax.rem(where[1] + CACHE - step, CACHE) * slot_total + slot
            rows = jnp.where(mine == holder, low, 0.0)
            key_low.append(jnp.where(for_key, rows, 0.0).astype(jnp.bfloat16))
            value_low.append(jnp.where(for_key, 0.0, rows).astype(jnp.bfloat16))
    key_low, value_low = jnp.concatenate(key_low, axis=1), jnp.concatenate(value_low, axis=1)
    up_rows = slot_total * low.shape[1]
    for head in range(out.shape[0]):
        cols = slice(head * HEAD, (head + 1) * HEAD)
        at = row_total + head * up_rows
        up = jnp.concatenate([m[at : at + up_rows, :] for m in messages], axis=0)
        out[head, 0:row_total, :] = (key[:, cols] + matmul(key_low, up)).astype(jnp.bfloat16)
        summed = value[:, cols] + matmul(value_low, up)
        for part in range(row_total // HEAD):
            rows = slice(part * HEAD, (part + 1) * HEAD)
            out[head, row_total + part * HEAD : row_total + (part + 1) * HEAD, :] = summed[
                rows, :
            ].T.astype(jnp.bfloat16)


def adapt(where, key, value, messages, slot_total):
    row_total, col_count = key.shape
    heads = col_count // HEAD
    return pl.pallas_call(
        functools.partial(adapt_kernel, slot_total),
        grid_spec=pltpu.PrefetchScalarGridSpec(
            num_scalar_prefetch=1,
            grid=(1,),
            in_specs=[whole(a.shape) for a in (key, value, *messages)],
            out_specs=whole((heads, 2 * row_total, HEAD)),
        ),
        out_shape=jax.ShapeDtypeStruct((heads, 2 * row_total, HEAD), jnp.bfloat16),
        compiler_params=pltpu.CompilerParams(vmem_limit_bytes=32 * 2**20),
        cost_estimate=pl.CostEstimate(flops=4 * 10**8, bytes_accessed=2 * 2**20, transcendentals=0),
    )(where, key, value, *messages)


def attend_kernel(first, last, backs, info, queries, span, *refs):
    at = 0
    blocks = []
    for back in backs:
        width = 2 if back == SEQ_Z // 2 else 1
        blocks.append(refs[at : at + width])
        at += width
    if not first:
        state_in, sums_in = refs[at : at + 2]
        at += 2
    outs = refs[at:]
    state, sums = outs[-2:]
    outs = outs[:-2]
    pair, head = pl.program_id(0), pl.program_id(1)
    columns = queries.shape[1]
    row_total = columns // 2
    if first:
        state[...] = jnp.zeros(state.shape, jnp.float32)
        sums[0:1, :] = jnp.full((1, columns), START, jnp.float32)
        sums[1:2, :] = jnp.zeros((1, columns), jnp.float32)
    else:
        state[...] = state_in[...]
        sums[...] = sums_in[...]
    a_first, a_last = info[4 * pair], info[4 * pair + 1]
    b_first, b_last = info[4 * pair + 2], info[4 * pair + 3]
    index = lax.broadcasted_iota(jnp.int32, (TAIL, row_total), 0)
    ones = jnp.where(index == 0, 1.0, 0.0).astype(jnp.bfloat16)

    def meets(back):
        key_first, key_last = info[8 + 3 * back], info[8 + 3 * back + 1]
        return ((key_first <= a_last) & (key_last >= a_first)) | (
            (key_first <= b_last) & (key_last >= b_first)
        )

    def visit(chosen):
        keys, values = [], []
        for which in chosen:
            block = blocks[which]
            if len(block) == 2:
                packed = jnp.where(head == 0, block[0][...], block[1][...])
            else:
                packed = block[0][head]
            keys.append(packed[0:row_total])
            turned = [packed[at : at + HEAD] for at in range(row_total, 2 * row_total, HEAD)]
            values.append(jnp.concatenate([jnp.concatenate(turned, axis=1), ones], axis=0))
        keys, values = jnp.concatenate(keys, axis=0), jnp.concatenate(values, axis=1)
        chains = [slice(at, at + 256) for at in range(0, columns, 256)]
        scores = [matmul(keys, queries[:, cols]) for cols in chains]
        weights = []
        for score, cols in zip(scores, chains):
            masked = []
            for place, which in enumerate(chosen):
                part = score[place * row_total : (place + 1) * row_total]
                places = info[8 + 3 * backs[which] + 2] + lax.broadcasted_iota(jnp.int32, part.shape, 0)
                inside = (places >= span[0:1, cols]) & (places < span[1:2, cols])
                masked.append(jnp.where(inside, part, NEG))
            old = sums[0:1, cols]
            top = functools.reduce(
                jnp.maximum, [old] + [jnp.max(part, axis=0, keepdims=True) for part in masked]
            )
            sums[0:1, cols] = top
            parts = [jnp.exp2(part - top).astype(jnp.bfloat16) for part in masked]
            weights.append((jnp.concatenate(parts, axis=0), jnp.exp2(old - top)))
        for (weight, factor), cols in zip(weights, chains):
            summed = matmul(values, weight)
            sums[1:2, cols] = sums[1:2, cols] * factor + summed[HEAD : HEAD + 1]
            state[:, cols] = state[:, cols] * factor + summed[0:HEAD]

    needed = [meets(back) for back in backs]
    for count in range(1, len(backs) + 1):
        for chosen in itertools.combinations(range(len(backs)), count):
            only = functools.reduce(
                jnp.logical_and,
                [need if which in chosen else jnp.logical_not(need) for which, need in enumerate(needed)],
            )

            @pl.when(only)
            def _(chosen=chosen):
                visit(chosen)

    if last:
        mass = sums[1:2, :]
        some = mass > 0.0
        filled = jnp.where(some, mass, 1.0)
        result = (state[...] * (1.0 / filled)).astype(jnp.bfloat16)
        logs = jnp.where(some, sums[0:1, :] + jnp.log2(filled), START)
        high = logs.astype(jnp.bfloat16).astype(jnp.float32)
        index = lax.broadcasted_iota(jnp.int32, (TAIL, columns), 0)
        tail = jnp.where(index == 0, high, logs - high).astype(jnp.bfloat16)
        for group, out in enumerate(outs):
            cols = slice(group % 2 * row_total, group % 2 * row_total + row_total)

            @pl.when(pair == group // 2)
            def _(out=out, cols=cols):
                out[0:HEAD, :] = result[:, cols]
                out[HEAD : HEAD + TAIL, :] = tail[:, cols]


def attend(info, queries, spans, blocks, state, last=False):
    first = state is None
    pairs, heads, _, columns = queries.shape
    row_total = columns // 2
    per_query = lambda rows: pl.BlockSpec((None, None, rows, columns), lambda p, h, s: (p, h, 0, 0))
    in_specs = [per_query(HEAD), pl.BlockSpec((None, 8, columns), lambda p, h, s: (p, 0, 0))]
    operands = [queries, spans]
    for arrays in blocks.values():
        in_specs += [whole(array.shape) for array in arrays]
        operands += list(arrays)
    if not first:
        in_specs += [per_query(HEAD), per_query(8)]
        operands += list(state)
    scratch = []
    if last:
        def place(pair):
            def index(p, h, s):
                return (jnp.where(p == pair, h, jnp.where(p < pair, 0, heads - 1)), 0, 0)

            return index

        out_shape = [jax.ShapeDtypeStruct((heads, HEAD + TAIL, row_total), jnp.bfloat16)] * SEQ_Y
        out_specs = [
            pl.BlockSpec((None, HEAD + TAIL, row_total), place(group // 2)) for group in range(SEQ_Y)
        ]
        scratch = [pltpu.VMEM((HEAD, columns), jnp.float32), pltpu.VMEM((8, columns), jnp.float32)]
    else:
        out_shape = [
            jax.ShapeDtypeStruct((pairs, heads, HEAD, columns), jnp.float32),
            jax.ShapeDtypeStruct((pairs, heads, 8, columns), jnp.float32),
        ]
        out_specs = [per_query(HEAD), per_query(8)]
    flops = ATTEND_FLOPS * len(blocks)
    return pl.pallas_call(
        functools.partial(attend_kernel, first, last, tuple(blocks)),
        grid_spec=pltpu.PrefetchScalarGridSpec(
            num_scalar_prefetch=1,
            grid=(pairs, heads),
            in_specs=in_specs,
            out_specs=out_specs,
            scratch_shapes=scratch,
        ),
        out_shape=out_shape,
        compiler_params=pltpu.CompilerParams(vmem_limit_bytes=24 * 2**20),
        cost_estimate=pl.CostEstimate(flops=flops, bytes_accessed=2**20, transcendentals=0),
    )(info, *operands)


def merge_kernel(*refs):
    out, parts = refs[-1], refs[:-1]
    for head in range(parts[0].shape[0]):
        logs = []
        for part in parts:
            tail = part[head, HEAD : HEAD + TAIL, :].astype(jnp.float32)
            logs.append(tail[0:1] + tail[1:2])
        top = functools.reduce(jnp.maximum, logs)
        shares = [jnp.exp2(log - top) for log in logs]
        scale = 1.0 / functools.reduce(jnp.add, shares)
        total = functools.reduce(
            jnp.add,
            [part[head, 0:HEAD, :].astype(jnp.float32) * (share * scale) for part, share in zip(parts, shares)],
        )
        out[:, head * HEAD : (head + 1) * HEAD] = total.T.astype(jnp.bfloat16)


def merge(parts):
    heads, rows, row_total = parts[0].shape
    return pl.pallas_call(
        merge_kernel,
        grid=(1,),
        in_specs=[whole(parts[0].shape)] * len(parts),
        out_specs=whole((row_total, heads * HEAD)),
        out_shape=jax.ShapeDtypeStruct((row_total, heads * HEAD), jnp.bfloat16),
        compiler_params=pltpu.CompilerParams(vmem_limit_bytes=40 * 2**20),
        cost_estimate=pl.CostEstimate(flops=10**6, bytes_accessed=2**20, transcendentals=0),
    )(*parts)


def output_kernel(where, *refs):
    out = refs[-1]
    count = (len(refs) - 1) // 2
    total = matmul(refs[0][...], refs[count][...])
    for rows, weight in zip(refs[1:count], refs[count + 1 : -1]):
        total = total + matmul(rows[...], weight[...])
    out[...] = total.astype(out.dtype)


def output(where, rows, weights, other, dtype):
    row_total, deep = rows[0].shape
    columns = weights[0].shape[1] // 2

    def side(i, where):
        return (0, 1 - where[2] if other else where[2])

    return pl.pallas_call(
        output_kernel,
        grid_spec=pltpu.PrefetchScalarGridSpec(
            num_scalar_prefetch=1,
            grid=(1,),
            in_specs=[whole((row_total, deep))] * len(rows)
            + [pl.BlockSpec((deep, columns), side)] * len(weights),
            out_specs=whole((row_total, columns)),
        ),
        out_shape=jax.ShapeDtypeStruct((row_total, columns), dtype),
        compiler_params=pltpu.CompilerParams(vmem_limit_bytes=40 * 2**20),
        cost_estimate=pl.CostEstimate(flops=3 * 10**8, bytes_accessed=2 * 2**20, transcendentals=0),
    )(where, *rows, *weights)


def per_device(
    tokens,
    query_weight,
    key_weight,
    value_weight,
    output_weight,
    adapter_down_maps,
    adapter_up_maps,
    request_lengths,
    request_adapter,
    adapter_slot,
):
    row_count = tokens.shape[0]
    col_count = query_weight.shape[1]
    slots_here = adapter_down_maps.shape[0]
    cache = lax.axis_index("cache")
    known = [jnp.stack([lax.axis_index("seq"), cache, lax.axis_index("mp")]).astype(jnp.int32)]
    known += [request_lengths, request_adapter, adapter_slot]
    known_total = sum(array.shape[0] for array in known)
    where, at = jnp.zeros((known_total,), jnp.int32), 0
    for array in known:
        where = where + jnp.pad(array, (at, known_total - at - array.shape[0]))
        at = at + array.shape[0]

    ups = adapter_up_maps.reshape(-1, adapter_up_maps.shape[3])
    *messages, spans, info = lower(where, tokens, adapter_down_maps, ups, col_count)
    tokens, *messages = lax.optimization_barrier((tokens, *messages))
    messages = [messages[0]] + [lax.ppermute(messages[s], "cache", around_x(s)) for s in (1, 2, 3)]
    key, value = project(tokens, key_weight, value_weight)
    tokens, key = lax.optimization_barrier((tokens, key))
    query = project_query(tokens, query_weight)
    groups = [query] + [lax.ppermute(query, "seq", around_y(s)) for s in (1, 2, 3)]
    queries = jnp.stack([jnp.concatenate(groups[0:2], axis=2), jnp.concatenate(groups[2:4], axis=2)])
    packed = adapt(where, key, value, messages, slots_here)

    output_weight, _ = lax.optimization_barrier((output_weight, packed))
    chip_cols = output_weight.shape[1] // CACHE

    def columns(step):
        return lax.dynamic_slice_in_dim(output_weight, (cache + step) % CACHE * chip_cols, chip_cols, 1)

    weights = [columns(0)] + [lax.ppermute(columns(s), "cache", around_x(s)) for s in (1, 2, 3)]

    def ring(right, left):
        return lax.ppermute(right, "seq", around_z(1)), lax.ppermute(left, "seq", around_z(-1))

    half = SEQ_Z // 2
    right_1, left_1 = ring(packed, packed)
    state = attend(info, queries, spans, {0: (packed,)}, None)
    right_1 = lax.optimization_barrier((state[0], right_1))[1]
    left_1 = lax.optimization_barrier((state[0], left_1))[1]
    right_2, left_2 = ring(right_1, left_1)
    state = attend(info, queries, spans, {1: (right_1,), SEQ_Z - 1: (left_1,)}, state)
    right_2 = lax.optimization_barrier((state[0], right_2))[1]
    left_2 = lax.optimization_barrier((state[0], left_2))[1]
    right_3, left_3 = ring(right_2, left_2)
    info, weights[1] = lax.optimization_barrier((info, weights[1]))
    state = attend(info, queries, spans, {2: (right_2,), SEQ_Z - 2: (left_2,)}, state)
    right_3 = lax.optimization_barrier((state[0], right_3))[1]
    left_3 = lax.optimization_barrier((state[0], left_3))[1]
    far = ring(right_3[0], left_3[1])
    info, weights[3] = lax.optimization_barrier((info, weights[3]))
    state = attend(info, queries, spans, {3: (right_3,), SEQ_Z - 3: (left_3,)}, state)
    parts = attend(info, queries, spans, {half: far}, state, last=True)

    parts = [parts[0]] + [lax.ppermute(parts[g], "seq", around_y(-g)) for g in (2, 1, 3)]
    *parts, weights[2] = lax.optimization_barrier((*parts, weights[2]))
    attended = merge(parts)
    rows = [attended] + [lax.ppermute(attended, "cache", around_x(s)) for s in (1, 2, 3)]
    theirs = output(where, rows, weights, True, jnp.bfloat16)
    theirs = lax.ppermute(theirs, "mp", [(0, 1), (1, 0)])
    mine = output(where, rows, weights, False, jnp.float32)
    return (mine + theirs.astype(jnp.float32)).astype(jnp.bfloat16)


def solution(mesh):
    placed = (
        P("seq", None),
        P(None, ("cache", "mp")),
        P(None, ("cache", "mp")),
        P(None, ("cache", "mp")),
        P(("cache", "mp"), None),
        P("cache", None, None),
        P("cache", None, None, None),
        P(),
        P(),
        P(),
    )
    return jax.shard_map(
        per_device, mesh=mesh, in_specs=placed, out_specs=P("seq", ("cache", "mp")), check_vma=False
    )
```

```python
import functools
import itertools
import math

import jax
import jax.numpy as jnp
from jax import lax
from jax.experimental import pallas as pl
from jax.experimental.pallas import tpu as pltpu
from jax.sharding import PartitionSpec as P

HEAD = 128
SEQ_Z = 8
SEQ_Y = 4
CACHE = 4
REQUESTS = 16
PLACES = 3
START = -1e30
NEG = -3e30
TAIL = 16
QUERY_SCALE = HEAD ** (-0.5) * math.log2(math.e)


CHUNKS = 2
ATTEND_FLOPS = 10**6


def around_z(step):
    return [
        (z * SEQ_Y + y, (z + step) % SEQ_Z * SEQ_Y + y) for z in range(SEQ_Z) for y in range(SEQ_Y)
    ]


def around_y(step):
    return [
        (z * SEQ_Y + y, z * SEQ_Y + (y + step) % SEQ_Y) for z in range(SEQ_Z) for y in range(SEQ_Y)
    ]


def around_x(step):
    return [(x, (x + step) % CACHE) for x in range(CACHE)]


def matmul(a, b, dims=((1,), (0,))):
    return lax.dot_general(a, b, (dims, ((), ())), preferred_element_type=jnp.float32)


def whole(shape):
    return pl.BlockSpec(shape, lambda *at: (0,) * len(shape))


def request_ends(known):
    bounds, at = [], jnp.int32(0)
    for r in range(REQUESTS):
        bounds.append((at, at + known[PLACES + r]))
        at = at + known[PLACES + r]
    return bounds


def slots_of_rows(places, known):
    found = jnp.zeros(places.shape, jnp.int32)
    for r, (start, _) in enumerate(request_ends(known)):
        found = jnp.where(places >= start, known[PLACES + 2 * REQUESTS + known[PLACES + REQUESTS + r]], found)
    return found


def requests_met(where, row_total, spans, info):
    bounds = request_ends(where)
    seq = where[0]
    seq_z, seq_y = lax.div(seq, SEQ_Y), lax.rem(seq, SEQ_Y)

    def request_at(row):
        found = jnp.int32(0)
        for _, end in bounds:
            found = found + (row >= end).astype(jnp.int32)
        return found

    def groups_row(group):
        return (seq_z * SEQ_Y + lax.rem(seq_y + SEQ_Y - group, SEQ_Y)) * row_total

    for group in range(SEQ_Y):
        row = groups_row(group)
        info[2 * group] = request_at(row)
        info[2 * group + 1] = request_at(row + row_total - 1)
        places = row + lax.broadcasted_iota(jnp.int32, (8, row_total), 1)
        starts = jnp.zeros(places.shape, jnp.int32)
        ends = jnp.zeros(places.shape, jnp.int32)
        for start, end in bounds:
            starts = jnp.where(places >= start, start, starts)
            ends = jnp.where(places >= start, end, ends)
        index = lax.broadcasted_iota(jnp.int32, (8, row_total), 0)
        cols = slice(group % 2 * row_total, group % 2 * row_total + row_total)
        spans[group // 2, :, cols] = jnp.where(index == 0, starts, ends)
    for back in range(SEQ_Z):
        row = (lax.rem(seq_z + SEQ_Z - back, SEQ_Z) * SEQ_Y + seq_y) * row_total
        info[8 + 3 * back] = request_at(row)
        info[8 + 3 * back + 1] = request_at(row + row_total - 1)
        info[8 + 3 * back + 2] = row


def lower_kernel(where, tokens, down, ups, *refs):
    outs, (spans, info, held, maps, columns, arrived) = refs[:CACHE], refs[CACHE:]
    row_total, width = tokens.shape
    slot_total, _, low = down.shape
    up_rows = ups.shape[0]
    col_count = columns.shape[2]
    deep = width // CHUNKS
    copies = []
    for chunk in range(CHUNKS):
        part = pl.ds(chunk * deep, deep)
        copies.append(
            [pltpu.make_async_copy(tokens.at[:, part], held.at[chunk], arrived.at[chunk * 4])]
            + [
                pltpu.make_async_copy(down.at[slot, part], maps.at[chunk, slot], arrived.at[chunk * 4 + 1 + slot])
                for slot in range(slot_total)
            ]
        )
    for chunk in range(CHUNKS):
        for copy in copies[chunk]:
            copy.start()
    up_copies = []
    for step in range(CACHE):
        first = pl.multiple_of((lax.rem(where[1] + step, CACHE) * 2 + where[2]) * col_count, HEAD)
        up_copies.append(
            pltpu.make_async_copy(ups.at[:, pl.ds(first, col_count)], columns.at[step], arrived.at[CHUNKS * 4 + step])
        )
        up_copies[-1].start()
    requests_met(where, row_total, spans, info)
    places = where[0] * row_total + lax.broadcasted_iota(jnp.int32, (row_total, low), 0)
    mine = slots_of_rows(places, where)
    total = None
    for chunk in range(CHUNKS):
        for copy in copies[chunk]:
            copy.wait()
        pair = jnp.concatenate([maps[chunk, slot] for slot in range(slot_total)], axis=1)
        product = matmul(held[chunk], pair)
        total = product if total is None else total + product
    rows = jnp.zeros((row_total, low), jnp.float32)
    for slot in range(slot_total):
        rows = jnp.where(
            mine == where[1] * slot_total + slot, total[:, slot * low : (slot + 1) * low], rows
        )
    rows = rows.astype(jnp.bfloat16)
    for step, out in enumerate(outs):
        up_copies[step].wait()
        out[0:row_total, :] = rows
        for half in range(col_count // HEAD):
            at = row_total + half * up_rows
            out[at : at + up_rows, :] = columns[step, :, half * HEAD : (half + 1) * HEAD]


def lower(where, tokens, down, ups, col_count):
    row_total, width = tokens.shape
    slot_total, _, low = down.shape
    up_rows = ups.shape[0]
    deep = width // CHUNKS
    out_rows = row_total + up_rows * col_count // HEAD
    return pl.pallas_call(
        lower_kernel,
        grid_spec=pltpu.PrefetchScalarGridSpec(
            num_scalar_prefetch=1,
            grid=(1,),
            in_specs=[pl.BlockSpec(memory_space=pltpu.HBM)] * 3,
            out_specs=[whole((out_rows, HEAD))] * CACHE
            + [whole((SEQ_Y // 2, 8, 2 * row_total)), pl.BlockSpec(memory_space=pltpu.SMEM)],
            scratch_shapes=[
                pltpu.VMEM((CHUNKS, row_total, deep), jnp.bfloat16),
                pltpu.VMEM((CHUNKS, slot_total, deep, low), jnp.bfloat16),
                pltpu.VMEM((CACHE, up_rows, col_count), jnp.bfloat16),
                pltpu.SemaphoreType.DMA((CHUNKS * 4 + CACHE,)),
            ],
        ),
        out_shape=[jax.ShapeDtypeStruct((out_rows, HEAD), jnp.bfloat16)] * CACHE
        + [
            jax.ShapeDtypeStruct((SEQ_Y // 2, 8, 2 * row_total), jnp.int32),
            jax.ShapeDtypeStruct((8 + 3 * SEQ_Z,), jnp.int32),
        ],
        compiler_params=pltpu.CompilerParams(vmem_limit_bytes=62 * 2**20),
        cost_estimate=pl.CostEstimate(flops=6 * 10**8, bytes_accessed=6 * 2**20, transcendentals=0),
    )(where, tokens, down, ups)


def query_kernel(steps, tokens, wq, query, total):
    step = pl.program_id(0)
    row_total = tokens.shape[0]
    held = tokens[...]

    @pl.when(step == 0)
    def _():
        total[...] = matmul(held, wq[...])

    @pl.when(step > 0)
    def _():
        total[...] += matmul(held, wq[...])

    @pl.when(step == steps - 1)
    def _():
        scaled = total[...] * QUERY_SCALE
        for head in range(query.shape[0]):
            query[head] = scaled[:, head * HEAD : (head + 1) * HEAD].T.astype(jnp.bfloat16)


def project_query(tokens, wq):
    steps = 3
    row_total, width = tokens.shape
    col_count = wq.shape[1]
    heads = col_count // HEAD
    deep = width // steps
    return pl.pallas_call(
        functools.partial(query_kernel, steps),
        grid=(steps,),
        in_specs=[
            pl.BlockSpec((row_total, deep), lambda i: (0, i)),
            pl.BlockSpec((deep, col_count), lambda i: (i, 0)),
        ],
        out_specs=whole((heads, HEAD, row_total)),
        scratch_shapes=[pltpu.VMEM((row_total, col_count), jnp.float32)],
        out_shape=jax.ShapeDtypeStruct((heads, HEAD, row_total), jnp.bfloat16),
        compiler_params=pltpu.CompilerParams(vmem_limit_bytes=24 * 2**20),
        cost_estimate=pl.CostEstimate(flops=6 * 10**8, bytes_accessed=4 * 2**20, transcendentals=0),
    )(tokens, wq)


def project_kernel(tokens, wk, wv, key, value):
    held = tokens[...]

    @pl.when(pl.program_id(0) == 0)
    def _():
        key[...] = matmul(held, wk[...])
        value[...] = matmul(held, wv[...])

    @pl.when(pl.program_id(0) > 0)
    def _():
        key[...] += matmul(held, wk[...])
        value[...] += matmul(held, wv[...])


def project(tokens, wk, wv):
    steps = 3
    row_total, width = tokens.shape
    col_count = wk.shape[1]
    deep = width // steps
    weight = pl.BlockSpec((deep, col_count), lambda i: (i, 0))
    summed = jax.ShapeDtypeStruct((row_total, col_count), jnp.float32)
    return pl.pallas_call(
        project_kernel,
        grid=(steps,),
        in_specs=[pl.BlockSpec((row_total, deep), lambda i: (0, i)), weight, weight],
        out_specs=[whole((row_total, col_count))] * 2,
        out_shape=[summed, summed],
        compiler_params=pltpu.CompilerParams(vmem_limit_bytes=24 * 2**20),
        cost_estimate=pl.CostEstimate(flops=12 * 10**8, bytes_accessed=6 * 2**20, transcendentals=0),
    )(tokens, wk, wv)


def adapt_kernel(slot_total, where, key, value, *refs):
    messages, out = refs[:-1], refs[-1]
    row_total = key.shape[0]
    low = functools.reduce(jnp.add, [m[0:row_total, :].astype(jnp.float32) for m in messages])
    places = where[0] * row_total + lax.broadcasted_iota(jnp.int32, low.shape, 0)
    mine = slots_of_rows(places, where)
    for_key = lax.broadcasted_iota(jnp.int32, low.shape, 1) < low.shape[1] // 2
    key_low, value_low = [], []
    for step in range(len(messages)):
        for slot in range(slot_total):
            holder = lax.rem(where[1] + CACHE - step, CACHE) * slot_total + slot
            rows = jnp.where(mine == holder, low, 0.0)
            key_low.append(jnp.where(for_key, rows, 0.0).astype(jnp.bfloat16))
            value_low.append(jnp.where(for_key, 0.0, rows).astype(jnp.bfloat16))
    key_low, value_low = jnp.concatenate(key_low, axis=1), jnp.concatenate(value_low, axis=1)
    up_rows = slot_total * low.shape[1]
    for head in range(out.shape[0]):
        cols = slice(head * HEAD, (head + 1) * HEAD)
        at = row_total + head * up_rows
        up = jnp.concatenate([m[at : at + up_rows, :] for m in messages], axis=0)
        out[head, 0:row_total, :] = (key[:, cols] + matmul(key_low, up)).astype(jnp.bfloat16)
        summed = value[:, cols] + matmul(value_low, up)
        for part in range(row_total // HEAD):
            rows = slice(part * HEAD, (part + 1) * HEAD)
            out[head, row_total + part * HEAD : row_total + (part + 1) * HEAD, :] = summed[
                rows, :
            ].T.astype(jnp.bfloat16)


def adapt(where, key, value, messages, slot_total):
    row_total, col_count = key.shape
    heads = col_count // HEAD
    return pl.pallas_call(
        functools.partial(adapt_kernel, slot_total),
        grid_spec=pltpu.PrefetchScalarGridSpec(
            num_scalar_prefetch=1,
            grid=(1,),
            in_specs=[whole(a.shape) for a in (key, value, *messages)],
            out_specs=whole((heads, 2 * row_total, HEAD)),
        ),
        out_shape=jax.ShapeDtypeStruct((heads, 2 * row_total, HEAD), jnp.bfloat16),
        compiler_params=pltpu.CompilerParams(vmem_limit_bytes=32 * 2**20),
        cost_estimate=pl.CostEstimate(flops=4 * 10**8, bytes_accessed=2 * 2**20, transcendentals=0),
    )(where, key, value, *messages)


def attend_kernel(first, last, backs, info, queries, span, *refs):
    at = 0
    blocks = []
    for back in backs:
        width = 2 if back == SEQ_Z // 2 else 1
        blocks.append(refs[at : at + width])
        at += width
    if not first:
        state_in, sums_in = refs[at : at + 2]
        at += 2
    outs = refs[at:]
    state, sums = outs[-2:]
    outs = outs[:-2]
    pair, head = pl.program_id(0), pl.program_id(1)
    columns = queries.shape[1]
    row_total = columns // 2
    if first:
        state[...] = jnp.zeros(state.shape, jnp.float32)
        sums[0:1, :] = jnp.full((1, columns), START, jnp.float32)
        sums[1:2, :] = jnp.zeros((1, columns), jnp.float32)
    else:
        state[...] = state_in[...]
        sums[...] = sums_in[...]
    a_first, a_last = info[4 * pair], info[4 * pair + 1]
    b_first, b_last = info[4 * pair + 2], info[4 * pair + 3]
    index = lax.broadcasted_iota(jnp.int32, (TAIL, row_total), 0)
    ones = jnp.where(index == 0, 1.0, 0.0).astype(jnp.bfloat16)

    def meets(back):
        key_first, key_last = info[8 + 3 * back], info[8 + 3 * back + 1]
        return ((key_first <= a_last) & (key_last >= a_first)) | (
            (key_first <= b_last) & (key_last >= b_first)
        )

    def visit(chosen):
        keys, values = [], []
        for which in chosen:
            block = blocks[which]
            if len(block) == 2:
                packed = jnp.where(head == 0, block[0][...], block[1][...])
            else:
                packed = block[0][head]
            keys.append(packed[0:row_total])
            turned = [packed[at : at + HEAD] for at in range(row_total, 2 * row_total, HEAD)]
            values.append(jnp.concatenate([jnp.concatenate(turned, axis=1), ones], axis=0))
        keys, values = jnp.concatenate(keys, axis=0), jnp.concatenate(values, axis=1)
        chains = [slice(at, at + 256) for at in range(0, columns, 256)]
        scores = [matmul(keys, queries[:, cols]) for cols in chains]
        weights = []
        for score, cols in zip(scores, chains):
            masked = []
            for place, which in enumerate(chosen):
                part = score[place * row_total : (place + 1) * row_total]
                places = info[8 + 3 * backs[which] + 2] + lax.broadcasted_iota(jnp.int32, part.shape, 0)
                inside = (places >= span[0:1, cols]) & (places < span[1:2, cols])
                masked.append(jnp.where(inside, part, NEG))
            old = sums[0:1, cols]
            top = functools.reduce(
                jnp.maximum, [old] + [jnp.max(part, axis=0, keepdims=True) for part in masked]
            )
            sums[0:1, cols] = top
            parts = [jnp.exp2(part - top).astype(jnp.bfloat16) for part in masked]
            weights.append((jnp.concatenate(parts, axis=0), jnp.exp2(old - top)))
        for (weight, factor), cols in zip(weights, chains):
            summed = matmul(values, weight)
            sums[1:2, cols] = sums[1:2, cols] * factor + summed[HEAD : HEAD + 1]
            state[:, cols] = state[:, cols] * factor + summed[0:HEAD]

    needed = [meets(back) for back in backs]
    for count in range(1, len(backs) + 1):
        for chosen in itertools.combinations(range(len(backs)), count):
            only = functools.reduce(
                jnp.logical_and,
                [need if which in chosen else jnp.logical_not(need) for which, need in enumerate(needed)],
            )

            @pl.when(only)
            def _(chosen=chosen):
                visit(chosen)

    if last:
        mass = sums[1:2, :]
        some = mass > 0.0
        filled = jnp.where(some, mass, 1.0)
        result = (state[...] * (1.0 / filled)).astype(jnp.bfloat16)
        logs = jnp.where(some, sums[0:1, :] + jnp.log2(filled), START)
        high = logs.astype(jnp.bfloat16).astype(jnp.float32)
        index = lax.broadcasted_iota(jnp.int32, (TAIL, columns), 0)
        tail = jnp.where(index == 0, high, logs - high).astype(jnp.bfloat16)
        for group, out in enumerate(outs):
            cols = slice(group % 2 * row_total, group % 2 * row_total + row_total)

            @pl.when(pair == group // 2)
            def _(out=out, cols=cols):
                out[0:HEAD, :] = result[:, cols]
                out[HEAD : HEAD + TAIL, :] = tail[:, cols]


def attend(info, queries, spans, blocks, state, last=False):
    first = state is None
    pairs, heads, _, columns = queries.shape
    row_total = columns // 2
    per_query = lambda rows: pl.BlockSpec((None, None, rows, columns), lambda p, h, s: (p, h, 0, 0))
    in_specs = [per_query(HEAD), pl.BlockSpec((None, 8, columns), lambda p, h, s: (p, 0, 0))]
    operands = [queries, spans]
    for arrays in blocks.values():
        in_specs += [whole(array.shape) for array in arrays]
        operands += list(arrays)
    if not first:
        in_specs += [per_query(HEAD), per_query(8)]
        operands += list(state)
    scratch = []
    if last:
        def place(pair):
            def index(p, h, s):
                return (jnp.where(p == pair, h, jnp.where(p < pair, 0, heads - 1)), 0, 0)

            return index

        out_shape = [jax.ShapeDtypeStruct((heads, HEAD + TAIL, row_total), jnp.bfloat16)] * SEQ_Y
        out_specs = [
            pl.BlockSpec((None, HEAD + TAIL, row_total), place(group // 2)) for group in range(SEQ_Y)
        ]
        scratch = [pltpu.VMEM((HEAD, columns), jnp.float32), pltpu.VMEM((8, columns), jnp.float32)]
    else:
        out_shape = [
            jax.ShapeDtypeStruct((pairs, heads, HEAD, columns), jnp.float32),
            jax.ShapeDtypeStruct((pairs, heads, 8, columns), jnp.float32),
        ]
        out_specs = [per_query(HEAD), per_query(8)]
    flops = ATTEND_FLOPS * len(blocks)
    return pl.pallas_call(
        functools.partial(attend_kernel, first, last, tuple(blocks)),
        grid_spec=pltpu.PrefetchScalarGridSpec(
            num_scalar_prefetch=1,
            grid=(pairs, heads),
            in_specs=in_specs,
            out_specs=out_specs,
            scratch_shapes=scratch,
        ),
        out_shape=out_shape,
        compiler_params=pltpu.CompilerParams(vmem_limit_bytes=24 * 2**20),
        cost_estimate=pl.CostEstimate(flops=flops, bytes_accessed=2**20, transcendentals=0),
    )(info, *operands)


def merge_kernel(*refs):
    out, parts = refs[-1], refs[:-1]
    for head in range(parts[0].shape[0]):
        logs = []
        for part in parts:
            tail = part[head, HEAD : HEAD + TAIL, :].astype(jnp.float32)
            logs.append(tail[0:1] + tail[1:2])
        top = functools.reduce(jnp.maximum, logs)
        shares = [jnp.exp2(log - top) for log in logs]
        scale = 1.0 / functools.reduce(jnp.add, shares)
        total = functools.reduce(
            jnp.add,
            [part[head, 0:HEAD, :].astype(jnp.float32) * (share * scale) for part, share in zip(parts, shares)],
        )
        out[:, head * HEAD : (head + 1) * HEAD] = total.T.astype(jnp.bfloat16)


def merge(parts):
    heads, rows, row_total = parts[0].shape
    return pl.pallas_call(
        merge_kernel,
        grid=(1,),
        in_specs=[whole(parts[0].shape)] * len(parts),
        out_specs=whole((row_total, heads * HEAD)),
        out_shape=jax.ShapeDtypeStruct((row_total, heads * HEAD), jnp.bfloat16),
        compiler_params=pltpu.CompilerParams(vmem_limit_bytes=40 * 2**20),
        cost_estimate=pl.CostEstimate(flops=10**6, bytes_accessed=2**20, transcendentals=0),
    )(*parts)


def output_kernel(where, *refs):
    out = refs[-1]
    count = (len(refs) - 1) // 2
    total = matmul(refs[0][...], refs[count][...])
    for rows, weight in zip(refs[1:count], refs[count + 1 : -1]):
        total = total + matmul(rows[...], weight[...])
    out[...] = total.astype(out.dtype)


def output(where, rows, weights, other, dtype):
    row_total, deep = rows[0].shape
    columns = weights[0].shape[1] // 2

    def side(i, where):
        return (0, 1 - where[2] if other else where[2])

    return pl.pallas_call(
        output_kernel,
        grid_spec=pltpu.PrefetchScalarGridSpec(
            num_scalar_prefetch=1,
            grid=(1,),
            in_specs=[whole((row_total, deep))] * len(rows)
            + [pl.BlockSpec((deep, columns), side)] * len(weights),
            out_specs=whole((row_total, columns)),
        ),
        out_shape=jax.ShapeDtypeStruct((row_total, columns), dtype),
        compiler_params=pltpu.CompilerParams(vmem_limit_bytes=40 * 2**20),
        cost_estimate=pl.CostEstimate(flops=3 * 10**8, bytes_accessed=2 * 2**20, transcendentals=0),
    )(where, *rows, *weights)


def per_device(
    tokens,
    query_weight,
    key_weight,
    value_weight,
    output_weight,
    adapter_down_maps,
    adapter_up_maps,
    request_lengths,
    request_adapter,
    adapter_slot,
):
    row_count = tokens.shape[0]
    col_count = query_weight.shape[1]
    slots_here = adapter_down_maps.shape[0]
    cache = lax.axis_index("cache")
    known = [jnp.stack([lax.axis_index("seq"), cache, lax.axis_index("mp")]).astype(jnp.int32)]
    known += [request_lengths, request_adapter, adapter_slot]
    known_total = sum(array.shape[0] for array in known)
    where, at = jnp.zeros((known_total,), jnp.int32), 0
    for array in known:
        where = where + jnp.pad(array, (at, known_total - at - array.shape[0]))
        at = at + array.shape[0]

    ups = adapter_up_maps.reshape(-1, adapter_up_maps.shape[3])
    *messages, spans, info = lower(where, tokens, adapter_down_maps, ups, col_count)
    tokens, *messages = lax.optimization_barrier((tokens, *messages))
    messages = [messages[0]] + [lax.ppermute(messages[s], "cache", around_x(s)) for s in (1, 2, 3)]
    key, value = project(tokens, key_weight, value_weight)
    tokens, key = lax.optimization_barrier((tokens, key))
    query = project_query(tokens, query_weight)
    groups = [query] + [lax.ppermute(query, "seq", around_y(s)) for s in (1, 2, 3)]
    queries = jnp.stack([jnp.concatenate(groups[0:2], axis=2), jnp.concatenate(groups[2:4], axis=2)])
    packed = adapt(where, key, value, messages, slots_here)

    output_weight, _ = lax.optimization_barrier((output_weight, packed))
    chip_cols = output_weight.shape[1] // CACHE

    def columns(step):
        return lax.dynamic_slice_in_dim(output_weight, (cache + step) % CACHE * chip_cols, chip_cols, 1)

    weights = [columns(0)] + [lax.ppermute(columns(s), "cache", around_x(s)) for s in (1, 2, 3)]

    def ring(right, left):
        return lax.ppermute(right, "seq", around_z(1)), lax.ppermute(left, "seq", around_z(-1))

    half = SEQ_Z // 2
    right_1, left_1 = ring(packed, packed)
    state = attend(info, queries, spans, {0: (packed,)}, None)
    right_1 = lax.optimization_barrier((state[0], right_1))[1]
    left_1 = lax.optimization_barrier((state[0], left_1))[1]
    right_2, left_2 = ring(right_1, left_1)
    state = attend(info, queries, spans, {1: (right_1,), SEQ_Z - 1: (left_1,)}, state)
    right_2 = lax.optimization_barrier((state[0], right_2))[1]
    left_2 = lax.optimization_barrier((state[0], left_2))[1]
    right_3, left_3 = ring(right_2, left_2)
    info, weights[2] = lax.optimization_barrier((info, weights[2]))
    state = attend(info, queries, spans, {2: (right_2,), SEQ_Z - 2: (left_2,)}, state)
    right_3 = lax.optimization_barrier((state[0], right_3))[1]
    left_3 = lax.optimization_barrier((state[0], left_3))[1]
    far = ring(right_3[0], left_3[1])
    info, weights[1], weights[3] = lax.optimization_barrier((info, weights[1], weights[3]))
    state = attend(info, queries, spans, {3: (right_3,), SEQ_Z - 3: (left_3,)}, state)
    parts = attend(info, queries, spans, {half: far}, state, last=True)

    parts = [parts[0]] + [lax.ppermute(parts[g], "seq", around_y(-g)) for g in (2, 1, 3)]
    attended = merge(parts)
    rows = [attended] + [lax.ppermute(attended, "cache", around_x(s)) for s in (1, 2, 3)]
    theirs = output(where, rows, weights, True, jnp.bfloat16)
    theirs = lax.ppermute(theirs, "mp", [(0, 1), (1, 0)])
    mine = output(where, rows, weights, False, jnp.float32)
    return (mine + theirs.astype(jnp.float32)).astype(jnp.bfloat16)


def solution(mesh):
    placed = (
        P("seq", None),
        P(None, ("cache", "mp")),
        P(None, ("cache", "mp")),
        P(None, ("cache", "mp")),
        P(("cache", "mp"), None),
        P("cache", None, None),
        P("cache", None, None, None),
        P(),
        P(),
        P(),
    )
    return jax.shard_map(
        per_device, mesh=mesh, in_specs=placed, out_specs=P("seq", ("cache", "mp")), check_vma=False
    )
```
